32 devices in a mesh: dp: 4 (over y, x), heads: 4 (over z), side: 2 (over core).
Axes of the slice: x: 2, y: 2, z: 4, core: 2. Of those that a mesh axis runs over, the one named last changes fastest.
Arguments:
- queries: bfloat16 [96, 2, 4096], P('dp', None, ('heads', 'side')), may hold values from -6 to 6
- new_keys: bfloat16 [96, 2, 4096], P('dp', None, ('heads', 'side')), may hold values from -6 to 6
- new_values: bfloat16 [96, 2, 4096], P('dp', None, ('heads', 'side')), may hold values from -6 to 6
- head_states: bfloat16 [96, 32, 128, 128], P('dp', ('heads', 'side')), may hold values from -6 to 6
- slopes: float32 [32], P(('heads', 'side')), may hold values from 0.004 to 0.9
- head_gain: float32 [4096], P(('heads', 'side')), may hold values from 0.5 to 1.5
- out_weight: bfloat16 [4096, 3072], P(('heads', 'side')), may hold values from -0.125 to 0.125
- residual: bfloat16 [96, 2, 3072], P('dp', None, ('heads', 'side')), may hold values from -10 to 10
- norm_gain: float32 [3072], replicated, may hold values from 0.5 to 1.5
- expert_ids: int32 [96, 2, 2], P('dp'), may hold values from 0 to 3, all different within a row; in each aligned block of 48 rows (0 to 47, 48 to 95, ..., all dimensions but the last counted through in order) at most 36 rows name the same one
- expert_gates: float32 [96, 2, 2], P('dp'), may hold values from 0.2 to 1
- w_gate: bfloat16 [4, 4, 768, 4608], P('dp', None, 'side', 'heads'), may hold values from -0.109375 to 0.109375
- w_up: bfloat16 [4, 4, 768, 4608], P('dp', None, 'side', 'heads'), may hold values from -0.109375 to 0.109375
- w_down: bfloat16 [4, 4608, 4, 768], P('dp', 'heads', None, 'side'), may hold values from -0.125 to 0.125
Outputs:
- state_out: bfloat16 [96, 32, 128, 128], P('dp', ('heads', 'side'))
- resid_out: bfloat16 [96, 2, 3072], P('dp', None, ('heads', 'side'))
- moe_out: bfloat16 [96, 2, 3072], P('dp', None, ('heads', 'side'))
The draws below stay inside these ranges and needn't reach their ends.
Inputs may be any that keep to these rules, and one draw needn't show every extreme that they name: `expert_ids`: among the 48 tokens of one dp index a token's 2 experts differ, no expert is chosen by more than 36 of them, and some expert is chosen by exactly 36.
All inputs are finite; a program needn't handle non-finite values.
Results may differ from the reference program's by a relative error of at most 0.025.
Values may be sent and summed in bfloat16 or wider, within the bound.
No kernel may reach another device: no remote copies, remote signals or barrier semaphores. Data moves between devices by JAX's collectives and lax.ppermute only.
A program may use at most 64 MiB of HBM per device.

```python
import math
import jax
import jax.numpy as jnp
import numpy as np
from jax import lax

D = 3072
HEADS = 32
HEAD = 128
FF = 4608
TOP = 2
STEPS = 2
REQUESTS = 96
EXPERTS = 4
D_GROUP = 768
T_DEV = 48
CAP = 36
N_DP = 4
N_HEADS = 4


def draw_residual(key, part):
    first_key = jax.random.fold_in(key, 0)
    columns = jnp.arange(D, dtype=jnp.float32) / D
    raw_values = jnp.clip(jax.random.normal(first_key, (REQUESTS, STEPS, D), jnp.float32), -5.0, 5.0)
    col_scale = 0.2 * jnp.exp(math.log(10.0) * columns)
    return (raw_values * col_scale).astype(jnp.bfloat16)


def strengthened(values, key, source, target, blocks, factor):
    owner, partner = [(jnp.arange(values.shape[axis_at]) // (values.shape[axis_at] // blocks)).reshape([-1 if axis == axis_at else 1 for axis in range(values.ndim)]) for axis_at in (source, target)]
    chosen = jax.random.permutation(key, blocks)[partner]
    strong = (owner == chosen) | (owner == (partner + blocks // 2) % blocks)
    return jnp.where(strong, factor * values, values)


def block_scale(key, dims, pieces, smallest, largest):
    level, own = 1.0, jax.random.fold_in(key, 6)
    for position, parts in pieces:
        heights = jnp.exp(jax.random.uniform(jax.random.fold_in(own, position), (parts,), jnp.float32, smallest / len(pieces), largest / len(pieces)))
        level = level * jnp.repeat(heights, dims[position] // parts).reshape([-1 if axis == position else 1 for axis in range(len(dims))])
    return level


def shared_out(rng, own, number, rows, number_of, top, bound, slope):
    ranking = jax.random.permutation(rng, number_of)
    crowded, common = shares(number_of, rows * top, bound, slope, True), shares(number_of, rows * top, bound, slope, False)
    places = jnp.arange(number_of)

    def named(lengths, offset_by):
        used = int((lengths > 0).sum())
        fixed = max(1, used // 4)
        shifted = fixed + (places - fixed + offset_by * (used - fixed)) % max(1, number_of - fixed)
        return jnp.zeros((number_of,), jnp.int32).at[ranking[jnp.where(places < fixed, places, shifted)]].set(jnp.asarray(lengths, jnp.int32))

    lengths = jnp.where(number % 4 == 0, named(crowded, number // 4), named(common, number - number // 4 - 1))
    mixed = jax.random.permutation(jax.random.fold_in(own, 3), number_of)
    donor, sink = mixed[0:number_of // 2 * 2:2], mixed[1:number_of // 2 * 2:2]
    room = jnp.minimum(lengths[donor] - 1, bound - lengths[sink]) // 2
    room = jnp.where((donor == ranking[0]) | (sink == ranking[0]) | (lengths[sink] == 0), 0, jnp.maximum(room, 0))
    shifted = jax.random.randint(jax.random.fold_in(own, 4), (number_of // 2,), 0, 1 << 20) % (room + 1)
    lengths = lengths.at[donor].add(-shifted).at[sink].add(shifted)
    labels = jnp.searchsorted(jnp.cumsum(lengths), jnp.arange(rows * top), side="right").astype(jnp.int32)
    table = labels.reshape(top, rows).T
    table = table[jax.random.permutation(jax.random.fold_in(own, 1), rows)]
    offset_by = jax.random.randint(jax.random.fold_in(own, 2), (rows, 1), 0, top)
    return jnp.take_along_axis(table, (jnp.arange(top)[None, :] + offset_by) % top, axis=1)


def shares(amount, total, limit, lean, full):
    portions = [(1 << 20) // math.isqrt(grade ** lean) + 1 for grade in range(1, amount + 1)]
    largest = limit if full else min(limit, max(-(-total // amount), total * portions[0] // sum(portions)))
    least = 1 if total - largest >= amount - 1 else 0
    holding, surplus = [largest] + [least] * (amount - 1), total - largest - least * (amount - 1)
    while surplus > 0:
        movable = [i for i in range(1, amount) if holding[i] < largest] or [i for i in range(1, amount) if holding[i] < limit]
        mass, budget = sum([portions[i] for i in movable]), surplus
        for i in movable:
            addition = min(limit - holding[i], max(1, budget * portions[i] // mass), surplus)
            holding[i] = holding[i] + addition
            surplus = surplus - addition
    return np.array(holding)


def scatter_about(stream_key, dims, deviation, bound, shards=(), kind=jnp.bfloat16):
    level = block_scale(stream_key, dims, shards, -0.22, 0.18) if shards else 1.0
    drawn = jax.random.normal(stream_key, dims, jnp.float32) * deviation * level
    return jnp.minimum(jnp.maximum(drawn, -bound), bound).astype(kind)


def bell_draw_with(stream_key, shape, scale, limit, cuts, heavy, kind=jnp.bfloat16):
    entries = scale * jax.random.normal(stream_key, shape, jnp.float32)
    if cuts:
        entries = entries * block_scale(stream_key, shape, cuts, -0.22, 0.18)
    return jnp.clip(strengthened(entries, jax.random.fold_in(stream_key, 3), *heavy), -limit, limit).astype(kind)


def setup_inputs(seed: int = 0) -> dict:
    key_list = jax.random.split(jax.random.key(seed), 15)
    queries = scatter_about(key_list[0], (REQUESTS, STEPS, HEADS * HEAD), 1.0, 6.0, ((0, 4), (2, 8)))
    new_keys = scatter_about(key_list[1], (REQUESTS, STEPS, HEADS * HEAD), 1.0, 6.0, ((0, 4), (2, 8)))
    new_values = scatter_about(key_list[2], (REQUESTS, STEPS, HEADS * HEAD), 1.0, 6.0, ((0, 4), (2, 8)))
    head_states = scatter_about(key_list[3], (REQUESTS, HEADS, HEAD, HEAD), 1.0, 6.0, ((0, 4), (1, 8)))
    slopes = jnp.clip(jnp.exp(math.log(0.9) - 5.4161003 * jax.random.uniform(key_list[4], (HEADS,), jnp.float32) ** block_scale(key_list[4], (HEADS,), ((0, 8),), -0.2, 0.2)), 0.004, 0.9)
    head_gain = jnp.clip(1.0 + 0.1 * jax.random.normal(key_list[5], (HEADS * HEAD,), jnp.float32), 0.5, 1.5)
    out_weight = bell_draw_with(key_list[6], (HEADS * HEAD, D), (HEADS * HEAD) ** -0.5, 0.125, ((0, 8),), (0, 1, 8, 2.0))
    residual = draw_residual(jax.random.fold_in(key_list[14], 71), 0)
    norm_gain = jnp.clip(1.0 + 0.1 * jax.random.normal(key_list[8], (D,), jnp.float32), 0.5, 1.5)
    expert_ids_keys = jax.random.split(jax.random.fold_in(key_list[9], 1), REQUESTS * STEPS // T_DEV)
    expert_ids_turns = jax.random.permutation(jax.random.fold_in(key_list[9], 3), REQUESTS * STEPS // T_DEV)
    expert_ids = jax.vmap(lambda own, number: shared_out(jax.random.fold_in(key_list[9], 2), own, number, T_DEV, EXPERTS, TOP, CAP, 2))(expert_ids_keys, expert_ids_turns).reshape((REQUESTS, STEPS, TOP))
    expert_gates = jnp.clip(jnp.exp(math.log(1.0) - 1.609438 * jax.random.uniform(key_list[10], (REQUESTS, STEPS, TOP), jnp.float32) ** block_scale(key_list[10], (REQUESTS, STEPS, TOP), ((0, 4),), -0.2, 0.2)), 0.2, 1.0)
    w_gate = scatter_about(key_list[11], (EXPERTS, N_HEADS, D_GROUP, FF), D ** -0.5, 0.109375, ((0, 4), (2, 2), (3, 4)))
    w_up = scatter_about(key_list[12], (EXPERTS, N_HEADS, D_GROUP, FF), D ** -0.5, 0.109375, ((0, 4), (2, 2), (3, 4)))
    w_down = bell_draw_with(key_list[13], (EXPERTS, FF, N_HEADS, D_GROUP), FF ** -0.5, 0.125, ((0, 4), (1, 4), (3, 2)), (1, 2, 4, 2.0))
    return {"queries": queries, "new_keys": new_keys, "new_values": new_values, "head_states": head_states, "slopes": slopes, "head_gain": head_gain, "out_weight": out_weight, "residual": residual, "norm_gain": norm_gain, "expert_ids": expert_ids, "expert_gates": expert_gates, "w_gate": w_gate, "w_up": w_up, "w_down": w_down}


def reference(queries, new_keys, new_values, head_states, slopes, head_gain, out_weight, residual, norm_gain, expert_ids, expert_gates, w_gate, w_up, w_down):
    query_rows = queries.astype(jnp.float32).reshape(REQUESTS, STEPS, HEADS, HEAD)
    key_rows = new_keys.astype(jnp.float32).reshape(REQUESTS, STEPS, HEADS, HEAD)
    value_rows = new_values.astype(jnp.float32).reshape(REQUESTS, STEPS, HEADS, HEAD)
    decays = jnp.exp(-slopes)[None, :, None, None]
    current = head_states.astype(jnp.float32)
    outputs = []
    for step in range(STEPS):
        current = decays * current + key_rows[:, step, :, :, None] * value_rows[:, step, :, None, :]
        outputs.append(jnp.einsum('rhi,rhij->rhj', query_rows[:, step], current, precision=lax.Precision.HIGHEST))
    state_out = current.astype(jnp.bfloat16)
    head_output = jnp.stack(outputs, 1)
    scaled = head_output * lax.rsqrt(lax.optimization_barrier(jnp.mean(head_output * head_output, -1, keepdims=True)) + 1e-06)
    normed = (scaled * head_gain.reshape(HEADS, HEAD)).astype(jnp.bfloat16).reshape(REQUESTS * STEPS, HEADS * HEAD)
    projected = jnp.dot(normed, out_weight, preferred_element_type=jnp.float32)
    resid_out = (residual.reshape(REQUESTS * STEPS, D).astype(jnp.float32) + projected).astype(jnp.bfloat16)
    stream = resid_out.astype(jnp.float32)
    mixed_in = (stream * lax.rsqrt(lax.optimization_barrier(jnp.mean(stream * stream, 1, keepdims=True)) + 1e-06) * norm_gain).astype(jnp.bfloat16)
    flat_ids = expert_ids.reshape(-1)
    token_index = jnp.arange(REQUESTS * STEPS * TOP, dtype=jnp.int32) // TOP
    most_rows = N_DP * CAP

    def one_expert(expert):
        chosen = flat_ids == expert
        ordering = jnp.argsort(jnp.where(chosen, 0, 1).astype(jnp.int32), stable=True)[:most_rows].astype(jnp.int32)
        inputs = mixed_in[token_index[ordering]]
        gate_matrix = w_gate[expert].reshape(D, FF)
        up_matrix = w_up[expert].reshape(D, FF)
        down_matrix = w_down[expert].reshape(FF, D)
        gate_val = jnp.dot(inputs, gate_matrix, preferred_element_type=jnp.float32)
        up_val = jnp.dot(inputs, up_matrix, preferred_element_type=jnp.float32)
        activation = (jax.nn.silu(gate_val) * up_val).astype(jnp.bfloat16)
        result = jnp.dot(activation, down_matrix, preferred_element_type=jnp.float32).astype(jnp.bfloat16)
        kept = jnp.where(chosen[ordering][:, None], result.astype(jnp.float32), jnp.zeros_like(result, dtype=jnp.float32))
        return (kept, ordering)
    results, orderings = lax.map(one_expert, jnp.arange(EXPERTS, dtype=jnp.int32))
    per_choice = jnp.zeros((REQUESTS * STEPS * TOP, D), jnp.float32).at[orderings.reshape(-1)].add(results.reshape(-1, D))
    weighted = per_choice * expert_gates.reshape(-1)[:, None]
    moe_out = lax.optimization_barrier(jnp.sum(weighted.reshape(REQUESTS * STEPS, TOP, D), 1)).astype(jnp.bfloat16)
    return (state_out, resid_out.reshape(REQUESTS, STEPS, D), moe_out.reshape(REQUESTS, STEPS, D))
```

```python
import functools

import jax
import jax.numpy as jnp
from jax import lax
from jax.experimental import pallas as pl
from jax.experimental.pallas import tpu as pltpu
from jax.sharding import PartitionSpec as P

BF = jnp.bfloat16
F32 = jnp.float32
VMEM_LIMIT = 48 * 1024 * 1024


def params():
    return pltpu.CompilerParams(vmem_limit_bytes=VMEM_LIMIT)


def struct(shape, dtype):
    return jax.ShapeDtypeStruct(shape, dtype)


def whole_vmem(count):
    return [pl.BlockSpec(memory_space=pltpu.VMEM)] * count


def cost(flops, size):
    return pl.CostEstimate(flops=flops, bytes_accessed=size, transcendentals=0)


def dot(a, b):
    return jnp.dot(a, b, preferred_element_type=F32)


def attention_kernel(
    slope_ref, q_ref, k_ref, v_ref, s_ref, gain_ref, w_hbm,
    so_ref, mine_ref, other_ref, normed, w_vmem, w_sem,
):
    step, steps = pl.program_id(0), pl.num_programs(0)
    copy = pltpu.make_async_copy(w_hbm, w_vmem, w_sem)

    @pl.when(step == 0)
    def _():
        copy.start()

    requests, tokens, width = q_ref.shape
    heads, size = s_ref.shape[1], s_ref.shape[2]
    rows = requests * tokens
    row = lax.broadcasted_iota(jnp.int32, (rows, size), 0)
    second = row % tokens == 1
    owner = row // tokens
    parts = []
    for h in range(heads):
        at = slice(h * size, (h + 1) * size)
        q16 = q_ref[:, :, at].reshape(rows, size)
        k16 = k_ref[:, :, at].reshape(rows, size)
        q, k = q16.astype(F32), k16.astype(F32)
        v = v_ref[:, :, at].reshape(rows, size).astype(F32)
        decay = jnp.exp(jnp.full((rows, size), -slope_ref[h], F32))
        read = jnp.zeros((rows, size), F32)
        for r in range(requests):
            read = jnp.where(owner == r, dot(q16, s_ref[r, h]), read)
        k_before = pltpu.roll(k, 1, 0)
        v_before = pltpu.roll(v, 1, 0)
        same = jnp.sum(q * k, -1, keepdims=True)
        cross = jnp.sum(q * k_before, -1, keepdims=True)
        out = jnp.where(second, decay * decay, decay) * read + same * v
        out = out + jnp.where(second, decay * cross * v_before, 0.0)
        out = out * lax.rsqrt(jnp.mean(out * out, -1, keepdims=True) + 1e-06)
        parts.append((out * gain_ref[:, at]).astype(BF))
        weighted = jnp.where(second, v, decay * v)
        spread = jnp.concatenate(
            [jnp.where(owner == r, weighted, 0.0).astype(BF) for r in range(requests)], 1
        )
        update = lax.dot_general(
            k16, spread, (((0,), (0,)), ((), ())), preferred_element_type=F32
        )
        keep = jnp.exp(jnp.full((size, size), -2.0 * slope_ref[h], F32))
        for r in range(requests):
            so_ref[r, h] = (
                keep * s_ref[r, h].astype(F32) + update[:, r * size : (r + 1) * size]
            ).astype(BF)
    block = jnp.concatenate(parts, 1) if heads > 1 else parts[0]
    normed[pl.ds(pl.multiple_of(step * rows, rows), rows), :] = block

    @pl.when(step == steps - 1)
    def _():
        copy.wait()
        side = lax.axis_index("side")
        groups, _, piece = mine_ref.shape
        for a in range(groups):
            both = dot(normed[...], w_vmem[:, 2 * a * piece : 2 * (a + 1) * piece])
            low, high = both[:, :piece], both[:, piece:]
            mine_ref[a] = jnp.where(side == 0, low, high)
            other_ref[a] = jnp.where(side == 0, high, low).astype(BF)


def attention(slopes, queries, new_keys, new_values, head_states, gain, out_weight, groups):
    requests, tokens, width = queries.shape
    heads, size = head_states.shape[1:3]
    block = 8 if requests % 8 == 0 else requests
    piece = out_weight.shape[1] // (2 * groups)
    rows = requests * tokens
    vec = pl.BlockSpec((block, tokens, width), lambda i: (i, 0, 0))
    state = pl.BlockSpec((block, heads, size, size), lambda i: (i, 0, 0, 0))
    fixed = pl.BlockSpec((groups, rows, piece), lambda i: (0, 0, 0))
    return pl.pallas_call(
        attention_kernel,
        grid=(requests // block,),
        in_specs=[
            pl.BlockSpec(memory_space=pltpu.SMEM),
            vec, vec, vec, state,
            pl.BlockSpec((1, width), lambda i: (0, 0)),
            pl.BlockSpec(memory_space=pl.ANY),
        ],
        out_specs=[state, fixed, fixed],
        out_shape=[
            struct(head_states.shape, BF),
            struct((groups, rows, piece), F32),
            struct((groups, rows, piece), BF),
        ],
        scratch_shapes=[
            pltpu.VMEM((rows, width), BF),
            pltpu.VMEM(out_weight.shape, BF),
            pltpu.SemaphoreType.DMA,
        ],
        compiler_params=params(),
        name="attention",
    )(slopes, queries, new_keys, new_values, head_states, gain, out_weight)


def split_kernel(mine_ref, recv_ref, own_ref, *send_refs):
    me = lax.axis_index("heads")
    own_ref[...] = mine_ref[me].astype(F32) + recv_ref[me].astype(F32)
    for k, send_ref in enumerate(send_refs, 1):
        at = me ^ k
        send_ref[...] = (mine_ref[at].astype(F32) + recv_ref[at].astype(F32)).astype(BF)


def split(mine, recv):
    groups, rows, piece = mine.shape
    return pl.pallas_call(
        split_kernel,
        in_specs=whole_vmem(2),
        out_specs=whole_vmem(groups),
        out_shape=[struct((rows, piece), F32)] + [struct((rows, piece), BF)] * (groups - 1),
        compiler_params=params(),
        name="split_sum",
    )(mine, recv)


def residual_kernel(residual_ref, own_ref, *refs):
    recv_refs, (resid_ref, flat_ref) = refs[:-2], refs[-2:]
    total = own_ref[...]
    for recv_ref in recv_refs:
        total = total + recv_ref[...].astype(F32)
    total = residual_ref[...].astype(F32).reshape(total.shape) + total
    rounded = total.astype(BF)
    flat_ref[...] = rounded
    resid_ref[...] = rounded.reshape(resid_ref.shape)


def add_residual(residual, own, recvs):
    return pl.pallas_call(
        residual_kernel,
        in_specs=whole_vmem(2 + len(recvs)),
        out_specs=whole_vmem(2),
        out_shape=[struct(residual.shape, BF), struct(own.shape, BF)],
        compiler_params=params(),
        name="add_residual",
    )(residual, own, *recvs)


def gate_up_kernel(gain_ref, wg_ref, wu_ref, *refs):
    x_refs, (out_ref, placed) = refs[:-2], refs[-2:]
    me, side = lax.axis_index("heads"), lax.axis_index("side")
    groups, rows, piece = x_refs[0].shape
    hidden = wg_ref.shape[3]
    total = rows * len(x_refs)
    squares = jnp.zeros((total, 1), F32)
    for k in range(groups):
        at = me ^ k
        x = jnp.concatenate([x_ref[k] for x_ref in x_refs], 0).astype(F32)
        squares = squares + jnp.sum(x * x, -1, keepdims=True)
        placed[at] = (x * gain_ref[pl.ds(at * 2 + side, 1), :]).astype(BF)
    lhs = jnp.concatenate([placed[a] for a in range(groups)], 1)
    wide = 384 if hidden % 384 == 0 else hidden
    for n in range(0, hidden, wide):
        rhs = wg_ref[0, :, :, n : n + wide].reshape(groups * piece, wide)
        out_ref[:, n : n + wide] = dot(lhs, rhs).astype(BF)
    for n in range(0, hidden, wide):
        rhs = wu_ref[0, :, :, n : n + wide].reshape(groups * piece, wide)
        out_ref[:, hidden + n : hidden + n + wide] = dot(lhs, rhs).astype(BF)
    coarse = squares.astype(BF)
    fine = (squares - coarse.astype(F32)).astype(BF)
    lane = lax.broadcasted_iota(jnp.int32, (total, 128), 1)
    extra = jnp.where(lane == 0, coarse.astype(F32), jnp.where(lane == 1, fine.astype(F32), 0.0))
    out_ref[:, 2 * hidden :] = extra.astype(BF)


def gate_up(gain, w_gate, w_up, xs):
    groups, rows, piece = xs[0].shape
    hidden = w_gate.shape[3]
    total = rows * len(xs)
    return pl.pallas_call(
        gate_up_kernel,
        in_specs=whole_vmem(3 + len(xs)),
        out_specs=pl.BlockSpec(memory_space=pltpu.VMEM),
        out_shape=struct((total, 2 * hidden + 128), BF),
        scratch_shapes=[pltpu.VMEM((groups, total, piece), BF)],
        compiler_params=params(),
        name="gate_up",
    )(gain, w_gate, w_up, *xs)


def regroup_kernel(w_ref, out_ref):
    count = w_ref.shape[1]
    step = 64 if count % 64 == 0 else 32

    def one(i, carry):
        at = pl.ds(pl.multiple_of(i * step, step), step)
        out_ref[:, at, :] = w_ref[0, at].swapaxes(0, 1)
        return carry

    lax.fori_loop(0, count // step, one, 0)


def regroup(w_down):
    _, hidden, groups, piece = w_down.shape
    return pl.pallas_call(
        regroup_kernel,
        in_specs=whole_vmem(1),
        out_specs=pl.BlockSpec(memory_space=pltpu.VMEM),
        out_shape=struct((groups, hidden, piece), BF),
        compiler_params=params(),
        name="regroup_down",
    )(w_down)


def down_kernel(width, part_ref, recv_ref, w_ref, *out_refs):
    groups, rows, piece = out_refs[0].shape
    hidden = w_ref.shape[1]
    extra = part_ref[:, 2 * hidden :].astype(F32) + recv_ref[:, 2 * hidden :].astype(F32)
    squares = extra[:, 0:1] + extra[:, 1:2]
    scale = lax.rsqrt(squares / width + 1e-06)
    gate = (part_ref[:, :hidden].astype(F32) + recv_ref[:, :hidden].astype(F32)) * scale
    up = (
        part_ref[:, hidden : 2 * hidden].astype(F32) + recv_ref[:, hidden : 2 * hidden].astype(F32)
    ) * scale
    act = (gate / (1.0 + jnp.exp(-gate)) * up).astype(BF)
    for a in range(groups):
        out = dot(act, w_ref[a]).astype(BF)
        for d, out_ref in enumerate(out_refs):
            out_ref[a] = out[d * rows : (d + 1) * rows]


def down(width, part, recv, weights, count):
    groups, hidden, piece = weights.shape
    rows = part.shape[0] // count
    return pl.pallas_call(
        functools.partial(down_kernel, width),
        in_specs=whole_vmem(3),
        out_specs=whole_vmem(count),
        out_shape=[struct((groups, rows, piece), BF)] * count,
        compiler_params=params(),
        name="down",
    )(part, recv, weights)


def combine_kernel(count, ids_ref, gates_ref, *refs):
    y_refs, out_refs = refs[:count], refs[count:]
    here, me = lax.axis_index("dp"), lax.axis_index("heads")
    groups, rows, piece = y_refs[0].shape
    tokens, choices, requests = ids_ref.shape
    row = lax.broadcasted_iota(jnp.int32, (rows, requests), 0)
    lane = lax.broadcasted_iota(jnp.int32, (rows, requests), 1)
    mine = [(row // tokens == lane) & (row % tokens == s) for s in range(tokens)]
    weights = []
    for d in range(count):
        weight = jnp.zeros((rows, requests), F32)
        for s in range(tokens):
            for c in range(choices):
                gate = jnp.where(
                    ids_ref[s, c : c + 1, :] == (here ^ d), gates_ref[s, c : c + 1, :], 0.0
                )
                weight = weight + jnp.where(mine[s], gate, 0.0)
        weights.append(jnp.sum(weight, -1, keepdims=True))
    for k, out_ref in enumerate(out_refs):
        at = me ^ k
        total = jnp.zeros((rows, piece), F32)
        for weight, y_ref in zip(weights, y_refs):
            total = total + weight * y_ref[at].astype(F32)
        out_ref[...] = total.astype(out_ref.dtype)


def combine(ids, gates, ys):
    groups, rows, piece = ys[0].shape
    return pl.pallas_call(
        functools.partial(combine_kernel, len(ys)),
        in_specs=whole_vmem(2 + len(ys)),
        out_specs=whole_vmem(groups),
        out_shape=[struct((rows, piece), F32)] + [struct((rows, piece), BF)] * (groups - 1),
        compiler_params=params(),
        name="combine",
    )(ids, gates, *ys)


def finish_kernel(own_ref, *refs):
    recv_refs, out_ref = refs[:-1], refs[-1]
    total = own_ref[...]
    for recv_ref in recv_refs:
        total = total + recv_ref[...].astype(F32)
    out_ref[...] = total.astype(BF).reshape(out_ref.shape)


def finish(own, recvs, shape):
    return pl.pallas_call(
        finish_kernel,
        in_specs=whole_vmem(1 + len(recvs)),
        out_specs=pl.BlockSpec(memory_space=pltpu.VMEM),
        out_shape=struct(shape, BF),
        compiler_params=params(),
        name="finish",
    )(own, *recvs)


def swap(x, axis, k):
    size = lax.axis_size(axis)
    return lax.ppermute(x, axis, [(i, i ^ k) for i in range(size)])


def local(
    queries, new_keys, new_values, head_states, slopes, head_gain, out_weight, residual,
    norm_gain, expert_ids, expert_gates, w_gate, w_up, w_down,
):
    groups, count = lax.axis_size("heads"), lax.axis_size("dp")
    width = norm_gain.shape[0]
    piece = residual.shape[2]
    state_out, mine, other = attention(
        slopes, queries, new_keys, new_values, head_states,
        head_gain.reshape(1, -1), out_weight, groups,
    )
    own, *sends = split(mine, swap(other, "side", 1))
    recvs = [swap(x, "heads", k) for k, x in enumerate(sends, 1)]
    resid_out, flat = add_residual(residual, own, recvs)
    gathered = jnp.stack([flat] + [swap(flat, "heads", k) for k in range(1, groups)])
    xs = [gathered] + [swap(gathered, "dp", k) for k in range(1, count)]
    part = gate_up(norm_gain.reshape(-1, piece), w_gate, w_up, xs)
    weights = regroup(w_down)
    own, *sends = down(width, part, swap(part, "side", 1), weights, count)
    ys = [own] + [swap(x, "dp", k) for k, x in enumerate(sends, 1)]
    own, *sends = combine(
        jnp.transpose(expert_ids, (1, 2, 0)), jnp.transpose(expert_gates, (1, 2, 0)), ys
    )
    recvs = [swap(x, "heads", k) for k, x in enumerate(sends, 1)]
    return state_out, resid_out, finish(own, recvs, residual.shape)


def solution(mesh):
    return jax.shard_map(
        local,
        mesh=mesh,
        in_specs=(
            P("dp", None, ("heads", "side")),
            P("dp", None, ("heads", "side")),
            P("dp", None, ("heads", "side")),
            P("dp", ("heads", "side"), None, None),
            P(("heads", "side")),
            P(("heads", "side")),
            P(("heads", "side"), None),
            P("dp", None, ("heads", "side")),
            P(),
            P("dp", None, None),
            P("dp", None, None),
            P("dp", None, "side", "heads"),
            P("dp", None, "side", "heads"),
            P("dp", "heads", None, "side"),
        ),
        out_specs=(
            P("dp", ("heads", "side"), None, None),
            P("dp", None, ("heads", "side")),
            P("dp", None, ("heads", "side")),
        ),
        check_vma=False,
    )
```

```python
import functools

import jax
import jax.numpy as jnp
from jax import lax
from jax.experimental import pallas as pl
from jax.experimental.pallas import tpu as pltpu
from jax.sharding import PartitionSpec as P

BF = jnp.bfloat16
F32 = jnp.float32
VMEM_LIMIT = 20 * 1024 * 1024
BIG_LIMIT = 58 * 1024 * 1024


def params(limit=VMEM_LIMIT):
    return pltpu.CompilerParams(vmem_limit_bytes=limit)


def struct(shape, dtype):
    return jax.ShapeDtypeStruct(shape, dtype)


def whole_vmem(count):
    return [pl.BlockSpec(memory_space=pltpu.VMEM)] * count


def cost(flops, size):
    return pl.CostEstimate(flops=flops, bytes_accessed=size, transcendentals=0)


def dot(a, b):
    return jnp.dot(a, b, preferred_element_type=F32)


def attention_kernel(
    slope_hbm, q_hbm, k_hbm, v_hbm, s_hbm, gain_hbm, w_hbm, mine_ref, other_ref,
    slope, q_all, k_all, v_all, states, gain, weight, small_sem, state_sem, weight_sem,
):
    small = [
        pltpu.make_async_copy(source, target, small_sem.at[i])
        for i, (source, target) in enumerate(
            ((q_hbm, q_all), (k_hbm, k_all), (v_hbm, v_all), (gain_hbm, gain), (slope_hbm, slope))
        )
    ]
    requests, tokens, _ = q_all.shape
    heads, size = states.shape[1], states.shape[2]
    block = 8 if requests % 8 == 0 else requests
    blocks = requests // block
    loads = [
        pltpu.make_async_copy(
            s_hbm.at[pl.ds(i * block, block)], states.at[pl.ds(i * block, block)], state_sem.at[i]
        )
        for i in range(blocks)
    ]
    weight_load = pltpu.make_async_copy(w_hbm, weight, weight_sem)
    for copy in small + loads + [weight_load]:
        copy.start()
    for copy in small:
        copy.wait()
    rows = block * tokens
    row = lax.broadcasted_iota(jnp.int32, (rows, size), 0)
    second = row % tokens == 1
    owner = row // tokens
    normed = []
    for i in range(blocks):
        loads[i].wait()
        parts = []
        for h in range(heads):
            at = slice(h * size, (h + 1) * size)
            here = slice(i * block, (i + 1) * block)
            q16 = q_all[here, :, at].reshape(rows, size)
            q = q16.astype(F32)
            k = k_all[here, :, at].reshape(rows, size).astype(F32)
            v = v_all[here, :, at].reshape(rows, size).astype(F32)
            decay = jnp.exp(jnp.full((rows, size), -slope[h], F32))
            read = jnp.zeros((rows, size), F32)
            for r in range(block):
                read = jnp.where(owner == r, dot(q16, states[i * block + r, h]), read)
            k_before = pltpu.roll(k, 1, 0)
            v_before = pltpu.roll(v, 1, 0)
            same = jnp.sum(q * k, -1, keepdims=True)
            cross = jnp.sum(q * k_before, -1, keepdims=True)
            out = jnp.where(second, decay * decay, decay) * read + same * v
            out = out + jnp.where(second, decay * cross * v_before, 0.0)
            out = out * lax.rsqrt(jnp.mean(out * out, -1, keepdims=True) + 1e-06)
            parts.append((out * gain[:, at]).astype(BF))
        normed.append(jnp.concatenate(parts, 1) if heads > 1 else parts[0])
    normed = jnp.concatenate(normed, 0) if blocks > 1 else normed[0]
    weight_load.wait()
    side = lax.axis_index("side")
    groups, _, piece = mine_ref.shape
    for a in range(groups):
        both = dot(normed, weight[:, 2 * a * piece : 2 * (a + 1) * piece])
        low, high = both[:, :piece], both[:, piece:]
        mine_ref[a] = jnp.where(side == 0, low, high)
        other_ref[a] = jnp.where(side == 0, high, low).astype(BF)


def attention(slopes, queries, new_keys, new_values, head_states, gain, out_weight, groups):
    requests, tokens, width = queries.shape
    piece = out_weight.shape[1] // (2 * groups)
    rows = requests * tokens
    vec = pltpu.VMEM(queries.shape, BF)
    return pl.pallas_call(
        attention_kernel,
        in_specs=[pl.BlockSpec(memory_space=pltpu.HBM)] * 7,
        out_specs=whole_vmem(2),
        out_shape=[struct((groups, rows, piece), F32), struct((groups, rows, piece), BF)],
        scratch_shapes=[
            pltpu.SMEM(slopes.shape, F32), vec, vec, vec,
            pltpu.VMEM(head_states.shape, BF),
            pltpu.VMEM(gain.shape, F32),
            pltpu.VMEM(out_weight.shape, BF),
            pltpu.SemaphoreType.DMA((5,)),
            pltpu.SemaphoreType.DMA((requests,)),
            pltpu.SemaphoreType.DMA,
        ],
        compiler_params=params(BIG_LIMIT),
        name="attention",
    )(slopes, queries, new_keys, new_values, head_states, gain, out_weight)


def state_kernel(slope_ref, k_ref, v_ref, s_ref, after_ref, so_ref, done_ref):
    del after_ref
    done_ref[...] = jnp.zeros_like(done_ref)
    requests, tokens, _ = k_ref.shape
    heads, size = s_ref.shape[1], s_ref.shape[2]
    rows = requests * tokens
    row = lax.broadcasted_iota(jnp.int32, (rows, size), 0)
    second = row % tokens == 1
    owner = row // tokens
    for h in range(heads):
        at = slice(h * size, (h + 1) * size)
        k16 = k_ref[:, :, at].reshape(rows, size)
        v = v_ref[:, :, at].reshape(rows, size).astype(F32)
        decay = jnp.exp(jnp.full((rows, size), -slope_ref[h], F32))
        weighted = jnp.where(second, v, decay * v)
        spread = jnp.concatenate(
            [jnp.where(owner == r, weighted, 0.0).astype(BF) for r in range(requests)], 1
        )
        update = lax.dot_general(
            k16, spread, (((0,), (0,)), ((), ())), preferred_element_type=F32
        )
        keep = jnp.exp(jnp.full((size, size), -2.0 * slope_ref[h], F32))
        for r in range(requests):
            so_ref[r, h] = (
                keep * s_ref[r, h].astype(F32) + update[:, r * size : (r + 1) * size]
            ).astype(BF)


def new_state(slopes, new_keys, new_values, head_states, after):
    requests, tokens, width = new_keys.shape
    heads, size = head_states.shape[1:3]
    block = 8 if requests % 8 == 0 else requests
    vec = pl.BlockSpec((block, tokens, width), lambda i: (i, 0, 0))
    state = pl.BlockSpec((block, heads, size, size), lambda i: (i, 0, 0, 0))
    return pl.pallas_call(
        state_kernel,
        grid=(requests // block,),
        in_specs=[
            pl.BlockSpec(memory_space=pltpu.SMEM), vec, vec, state,
            pl.BlockSpec(memory_space=pl.ANY),
        ],
        out_specs=[state, pl.BlockSpec((8, 128), lambda i: (0, 0))],
        out_shape=[struct(head_states.shape, BF), struct((8, 128), F32)],
        compiler_params=params(),
        cost_estimate=cost(10**8, 8 * 10**6),
        name="new_state",
    )(slopes, new_keys, new_values, head_states, after)


def hold_kernel(x_ref, out_ref):
    out_ref[...] = x_ref[...]


def hold(x):
    return pl.pallas_call(
        hold_kernel,
        in_specs=whole_vmem(1),
        out_specs=pl.BlockSpec(memory_space=pltpu.VMEM),
        out_shape=struct(x.shape, x.dtype),
        compiler_params=params(),
        cost_estimate=cost(10**5, 10**6),
        name="hold",
    )(x)


def split_kernel(mine_ref, recv_ref, own_ref, *send_refs):
    me = lax.axis_index("heads")
    own_ref[...] = mine_ref[me].astype(F32) + recv_ref[me].astype(F32)
    for k, send_ref in zip(range(len(send_refs), 0, -1), send_refs):
        at = me ^ k
        send_ref[...] = (mine_ref[at].astype(F32) + recv_ref[at].astype(F32)).astype(BF)


def split(mine, recv):
    groups, rows, piece = mine.shape
    return pl.pallas_call(
        split_kernel,
        in_specs=whole_vmem(2),
        out_specs=whole_vmem(groups),
        out_shape=[struct((rows, piece), F32)] + [struct((rows, piece), BF)] * (groups - 1),
        compiler_params=params(),
        name="split_sum",
    )(mine, recv)


def residual_kernel(residual_ref, after_ref, own_ref, *refs):
    del after_ref
    recv_refs, flat_ref = refs[:-1], refs[-1]
    total = own_ref[...]
    for recv_ref in recv_refs:
        total = total + recv_ref[...].astype(F32)
    total = residual_ref[...].astype(F32).reshape(total.shape) + total
    flat_ref[...] = total.astype(BF)


def add_residual(residual, after, own, recvs):
    return pl.pallas_call(
        residual_kernel,
        in_specs=[whole_vmem(1)[0], pl.BlockSpec(memory_space=pl.ANY)] + whole_vmem(1 + len(recvs)),
        out_specs=pl.BlockSpec(memory_space=pltpu.VMEM),
        out_shape=struct(own.shape, BF),
        compiler_params=params(),
        name="add_residual",
    )(residual, after, own, *recvs)


def reshape_kernel(flat_ref, out_ref):
    out_ref[...] = flat_ref[...].reshape(out_ref.shape)


def by_request(flat, shape):
    return pl.pallas_call(
        reshape_kernel,
        in_specs=whole_vmem(1),
        out_specs=pl.BlockSpec(memory_space=pltpu.VMEM),
        out_shape=struct(shape, BF),
        compiler_params=params(),
        cost_estimate=cost(10**5, 10**6),
        name="by_request",
    )(flat)


def route_kernel(capacity, ids_ref, gates_ref, after_ref, pick_ref, high_ref, low_ref):
    del after_ref
    here = lax.axis_index("dp")
    tokens, choices, requests = ids_ref.shape
    rows, total = pick_ref.shape
    row = lax.broadcasted_iota(jnp.int32, (rows, requests), 0)
    lane = lax.broadcasted_iota(jnp.int32, (rows, requests), 1)
    mine = [(row // tokens == lane) & (row % tokens == s) for s in range(tokens)]
    ids, gates = [], []
    for c in range(choices):
        number, gate = jnp.zeros((rows, requests), jnp.int32), jnp.zeros((rows, requests), F32)
        for s in range(tokens):
            number = number + jnp.where(mine[s], ids_ref[s, c : c + 1, :], 0)
            gate = gate + jnp.where(mine[s], gates_ref[s, c : c + 1, :], 0.0)
        ids.append(jnp.sum(number.astype(F32), -1, keepdims=True).astype(jnp.int32))
        gates.append(jnp.sum(gate, -1, keepdims=True))
    column = lax.broadcasted_iota(jnp.int32, (rows, total), 1)
    expert = here ^ (column // capacity)
    chosen, weight = jnp.zeros((rows, total), F32), jnp.zeros((rows, total), F32)
    for c in range(choices):
        named = ids[c] == expert
        chosen = jnp.where(named, 1.0, chosen)
        weight = jnp.where(named, gates[c], weight)
    earlier = lax.broadcasted_iota(jnp.int32, (rows, rows), 1) < lax.broadcasted_iota(
        jnp.int32, (rows, rows), 0
    )
    place = dot(jnp.where(earlier, 1.0, 0.0).astype(BF), chosen.astype(BF))
    hit = (chosen > 0.5) & (place.astype(jnp.int32) == column % capacity)
    pick_ref[...] = jnp.where(hit, 1.0, 0.0).astype(BF)
    weight = jnp.where(hit, weight, 0.0)
    high = weight.astype(BF)
    high_ref[...] = high
    low_ref[...] = (weight - high.astype(F32)).astype(BF)


def route(ids, gates, after, capacity, count):
    rows = ids.shape[0] * ids.shape[2]
    return pl.pallas_call(
        functools.partial(route_kernel, capacity),
        in_specs=whole_vmem(2) + [pl.BlockSpec(memory_space=pl.ANY)],
        out_specs=whole_vmem(3),
        out_shape=[struct((rows, count * capacity), BF)] * 3,
        compiler_params=params(),
        cost_estimate=cost(10**5, 10**6),
        name="route",
    )(ids, gates, after)


def dispatch_kernel(count, pick_ref, *refs):
    x_refs, out_refs = refs[:-count], refs[-count:]
    capacity = out_refs[0].shape[0] // len(x_refs)
    picked = [
        lax.dot_general(
            pick_ref[...], x_ref[...], (((0,), (0,)), ((), ())), preferred_element_type=F32
        )
        for x_ref in x_refs
    ]
    for k, out_ref in zip((0, *range(count - 1, 0, -1)), out_refs):
        rows = [x[k * capacity : (k + 1) * capacity] for x in picked]
        out_ref[...] = jnp.concatenate(rows, 0).astype(BF)


def dispatch(pick, xs, count):
    piece = xs[0].shape[1]
    rows = len(xs) * pick.shape[1] // count
    return pl.pallas_call(
        functools.partial(dispatch_kernel, count),
        in_specs=whole_vmem(1 + len(xs)),
        out_specs=whole_vmem(count),
        out_shape=[struct((rows, piece), BF)] * count,
        compiler_params=params(),
        name="dispatch",
    )(pick, *xs)


def gate_up_kernel(gain_ref, wg_ref, wu_ref, after_ref, *refs):
    del after_ref
    x_refs, (out_ref, placed) = refs[:-2], refs[-2:]
    me, side = lax.axis_index("heads"), lax.axis_index("side")
    groups, total, piece = placed.shape
    hidden = wg_ref.shape[3]
    capacity = total // len(x_refs)
    squares = jnp.zeros((total, 1), F32)
    xs = [x_ref[...].astype(F32) for x_ref in x_refs]
    for k in range(groups):
        at = me ^ k
        x = jnp.concatenate([x[k * capacity : (k + 1) * capacity] for x in xs], 0)
        squares = squares + jnp.sum(x * x, -1, keepdims=True)
        placed[at] = (x * gain_ref[pl.ds(at * 2 + side, 1), :]).astype(BF)
    lhs = jnp.concatenate([placed[a] for a in range(groups)], 1)
    wide = 384 if hidden % 384 == 0 else hidden
    for n in range(0, hidden, wide):
        rhs = wg_ref[0, :, :, n : n + wide].reshape(groups * piece, wide)
        out_ref[:, n : n + wide] = dot(lhs, rhs).astype(BF)
    for n in range(0, hidden, wide):
        rhs = wu_ref[0, :, :, n : n + wide].reshape(groups * piece, wide)
        out_ref[:, hidden + n : hidden + n + wide] = dot(lhs, rhs).astype(BF)
    coarse = squares.astype(BF)
    fine = (squares - coarse.astype(F32)).astype(BF)
    lane = lax.broadcasted_iota(jnp.int32, (total, 128), 1)
    extra = jnp.where(lane == 0, coarse.astype(F32), jnp.where(lane == 1, fine.astype(F32), 0.0))
    out_ref[:, 2 * hidden :] = extra.astype(BF)


def gate_up(gain, w_gate, w_up, after, xs):
    _, groups, piece, hidden = w_gate.shape
    total = xs[0].shape[0] // groups * len(xs)
    return pl.pallas_call(
        gate_up_kernel,
        in_specs=whole_vmem(3) + [pl.BlockSpec(memory_space=pl.ANY)] + whole_vmem(len(xs)),
        out_specs=pl.BlockSpec(memory_space=pltpu.VMEM),
        out_shape=struct((total, 2 * hidden + 128), BF),
        scratch_shapes=[pltpu.VMEM((groups, total, piece), BF)],
        compiler_params=params(),
        name="gate_up",
    )(gain, w_gate, w_up, after, *xs)


def regroup_kernel(w_ref, after_ref, out_ref):
    del after_ref
    count = w_ref.shape[1]
    step = 64 if count % 64 == 0 else 32

    def one(i, carry):
        at = pl.ds(pl.multiple_of(i * step, step), step)
        out_ref[:, at, :] = w_ref[0, at].swapaxes(0, 1)
        return carry

    lax.fori_loop(0, count // step, one, 0)


def regroup(w_down, after):
    _, hidden, groups, piece = w_down.shape
    return pl.pallas_call(
        regroup_kernel,
        in_specs=[whole_vmem(1)[0], pl.BlockSpec(memory_space=pl.ANY)],
        out_specs=pl.BlockSpec(memory_space=pltpu.VMEM),
        out_shape=struct((groups, hidden, piece), BF),
        compiler_params=params(),
        cost_estimate=cost(10**8, 7 * 10**6),
        name="regroup_down",
    )(w_down, after)


def down_kernel(width, part_ref, recv_ref, w_ref, *out_refs):
    groups, hidden, piece = w_ref.shape
    capacity = part_ref.shape[0] // len(out_refs)
    extra = part_ref[:, 2 * hidden :].astype(F32) + recv_ref[:, 2 * hidden :].astype(F32)
    squares = extra[:, 0:1] + extra[:, 1:2]
    scale = lax.rsqrt(squares / width + 1e-06)
    gate = (part_ref[:, :hidden].astype(F32) + recv_ref[:, :hidden].astype(F32)) * scale
    up = (
        part_ref[:, hidden : 2 * hidden].astype(F32) + recv_ref[:, hidden : 2 * hidden].astype(F32)
    ) * scale
    act = (gate / (1.0 + jnp.exp(-gate)) * up).astype(BF)
    outs = [dot(act, w_ref[a]) for a in range(groups)]
    for d, out_ref in zip((0, *range(len(out_refs) - 1, 0, -1)), out_refs):
        rows = [out[d * capacity : (d + 1) * capacity] for out in outs]
        out_ref[...] = jnp.concatenate(rows, 0).astype(BF)


def down(width, part, recv, weights, count):
    groups, hidden, piece = weights.shape
    rows = part.shape[0] // count * groups
    return pl.pallas_call(
        functools.partial(down_kernel, width),
        in_specs=whole_vmem(3),
        out_specs=whole_vmem(count),
        out_shape=[struct((rows, piece), BF)] * count,
        compiler_params=params(),
        name="down",
    )(part, recv, weights)


def combine_kernel(count, high_ref, low_ref, *refs):
    y_refs, out_refs, total = refs[:count], refs[count:-1], refs[-1]
    me = lax.axis_index("heads")
    groups = total.shape[0]
    capacity = y_refs[0].shape[0] // groups
    ys = [y_ref[...].astype(F32) for y_ref in y_refs]
    for a in range(groups):
        y = jnp.concatenate([y[a * capacity : (a + 1) * capacity] for y in ys], 0).astype(BF)
        total[a] = dot(high_ref[...], y) + dot(low_ref[...], y)
    for k, out_ref in zip((0, *range(groups - 1, 0, -1)), out_refs):
        out_ref[...] = total[me ^ k].astype(out_ref.dtype)


def combine(high, low, ys, groups):
    rows, piece = high.shape[0], ys[0].shape[1]
    return pl.pallas_call(
        functools.partial(combine_kernel, len(ys)),
        in_specs=whole_vmem(2 + len(ys)),
        out_specs=whole_vmem(groups),
        out_shape=[struct((rows, piece), F32)] + [struct((rows, piece), BF)] * (groups - 1),
        scratch_shapes=[pltpu.VMEM((groups, rows, piece), F32)],
        compiler_params=params(),
        name="combine",
    )(high, low, *ys)


def finish_kernel(own_ref, *refs):
    recv_refs, out_ref = refs[:-1], refs[-1]
    total = own_ref[...]
    for recv_ref in recv_refs:
        total = total + recv_ref[...].astype(F32)
    out_ref[...] = total.astype(BF).reshape(out_ref.shape)


def finish(own, recvs, shape):
    return pl.pallas_call(
        finish_kernel,
        in_specs=whole_vmem(1 + len(recvs)),
        out_specs=pl.BlockSpec(memory_space=pltpu.VMEM),
        out_shape=struct(shape, BF),
        compiler_params=params(),
        name="finish",
    )(own, *recvs)


def swap(x, axis, k):
    size = lax.axis_size(axis)
    return lax.ppermute(x, axis, [(i, i ^ k) for i in range(size)])


def swaps(sends, axis):
    return [swap(x, axis, k) for k, x in zip(range(len(sends), 0, -1), sends)]


def local(
    queries, new_keys, new_values, head_states, slopes, head_gain, out_weight, residual,
    norm_gain, expert_ids, expert_gates, w_gate, w_up, w_down,
):
    groups, count = lax.axis_size("heads"), lax.axis_size("dp")
    width = norm_gain.shape[0]
    piece = residual.shape[2]
    mine, other = attention(
        slopes, queries, new_keys, new_values, head_states,
        head_gain.reshape(1, -1), out_weight, groups,
    )
    own, *sends = split(hold(mine), swap(other, "side", 1))
    recvs = swaps(sends, "heads")
    state_out, done = new_state(slopes, new_keys, new_values, head_states, own)
    flat = add_residual(residual, done, own, recvs)
    resid_out = by_request(flat, residual.shape)
    capacity = max(2, 3 * expert_ids.shape[2] * flat.shape[0] // (2 * count))
    pick, high, low = route(
        jnp.transpose(expert_ids, (1, 2, 0)), jnp.transpose(expert_gates, (1, 2, 0)), done,
        capacity, count,
    )
    gathered = [flat] + swaps([flat] * (groups - 1), "heads")[::-1]
    own, *sends = dispatch(pick, gathered, count)
    xs = [own] + swaps(sends, "dp")[::-1]
    weights = regroup(w_down, own)
    part = gate_up(norm_gain.reshape(-1, piece), w_gate, w_up, weights, xs)
    own, *sends = down(width, part, swap(part, "side", 1), weights, count)
    ys = [own] + swaps(sends, "dp")[::-1]
    own, *sends = combine(high, low, ys, groups)
    return state_out, resid_out, finish(own, swaps(sends, "heads"), residual.shape)


def solution(mesh):
    return jax.shard_map(
        local,
        mesh=mesh,
        in_specs=(
            P("dp", None, ("heads", "side")),
            P("dp", None, ("heads", "side")),
            P("dp", None, ("heads", "side")),
            P("dp", ("heads", "side"), None, None),
            P(("heads", "side")),
            P(("heads", "side")),
            P(("heads", "side"), None),
            P("dp", None, ("heads", "side")),
            P(),
            P("dp", None, None),
            P("dp", None, None),
            P("dp", None, "side", "heads"),
            P("dp", None, "side", "heads"),
            P("dp", "heads", None, "side"),
        ),
        out_specs=(
            P("dp", ("heads", "side"), None, None),
            P("dp", None, ("heads", "side")),
            P("dp", None, ("heads", "side")),
        ),
        check_vma=False,
    )
```

```python
import functools

import jax
import jax.numpy as jnp
from jax import lax
from jax.experimental import pallas as pl
from jax.experimental.pallas import tpu as pltpu
from jax.sharding import PartitionSpec as P

BF = jnp.bfloat16
F32 = jnp.float32
VMEM_LIMIT = 20 * 1024 * 1024
BIG_LIMIT = 58 * 1024 * 1024


def params(limit=VMEM_LIMIT):
    return pltpu.CompilerParams(vmem_limit_bytes=limit)


def struct(shape, dtype):
    return jax.ShapeDtypeStruct(shape, dtype)


def in_vmem(shape, dtype):
    return pltpu.VMEM(shape, dtype)


def from_hbm(x):
    return pltpu.with_memory_space_constraint(x, pltpu.HBM)


def hbm_specs(count):
    return [pl.BlockSpec(memory_space=pltpu.HBM)] * count


def whole_vmem(count):
    return [pl.BlockSpec(memory_space=pltpu.VMEM)] * count


def cost(flops, size):
    return pl.CostEstimate(flops=flops, bytes_accessed=size, transcendentals=0)


def dot(a, b):
    return jnp.dot(a, b, preferred_element_type=F32)


def load_columns(w_hbm, weight, sems, side):
    groups, _, piece = weight.shape
    if groups == 1:
        return [pltpu.make_async_copy(w_hbm, weight.at[0], sems.at[0])]
    return [
        pltpu.make_async_copy(
            w_hbm.at[:, pl.ds(pl.multiple_of((2 * a + side) * piece, 128), piece)],
            weight.at[a],
            sems.at[a],
        )
        for a in range(groups)
    ]


def columns_shape(out_weight, groups):
    rows, width = out_weight.shape
    piece = width // (2 * groups)
    return (groups, rows, piece) if piece % 128 == 0 else (1, rows, width)


def project_columns(loads, weight, normed, side, out_ref):
    groups, _, piece = out_ref.shape
    if len(loads) == groups:
        for a, copy in enumerate(loads):
            copy.wait()
            out_ref[a] = dot(normed, weight[a]).astype(out_ref.dtype)
        return
    loads[0].wait()
    for a in range(groups):
        both = dot(normed, weight[0, :, 2 * a * piece : 2 * (a + 1) * piece])
        out = jnp.where(side == 0, both[:, :piece], both[:, piece:])
        out_ref[a] = out.astype(out_ref.dtype)


def attention_kernel(
    slope_hbm, q_hbm, k_hbm, v_hbm, s_hbm, gain_hbm, w_hbm, other_ref, normed_ref, states,
    slope, q_all, k_all, v_all, gain, weight, small_sem, state_sem, weight_sem,
):
    small = [
        pltpu.make_async_copy(source, target, small_sem.at[i])
        for i, (source, target) in enumerate(
            ((q_hbm, q_all), (k_hbm, k_all), (v_hbm, v_all), (gain_hbm, gain), (slope_hbm, slope))
        )
    ]
    requests, tokens, _ = q_all.shape
    heads, size = states.shape[1], states.shape[2]
    block = 8 if requests % 8 == 0 else requests
    blocks = requests // block
    loads = [
        pltpu.make_async_copy(
            s_hbm.at[pl.ds(i * block, block)], states.at[pl.ds(i * block, block)], state_sem.at[i]
        )
        for i in range(blocks)
    ]
    weight_loads = load_columns(w_hbm, weight, weight_sem, 1 - lax.axis_index("side"))
    for copy in small + loads + weight_loads:
        copy.start()
    for copy in small:
        copy.wait()
    rows = block * tokens
    row = lax.broadcasted_iota(jnp.int32, (rows, size), 0)
    second = row % tokens == 1
    owner = row // tokens
    normed = []
    for i in range(blocks):
        loads[i].wait()
        parts = []
        for h in range(heads):
            at = slice(h * size, (h + 1) * size)
            here = slice(i * block, (i + 1) * block)
            q16 = q_all[here, :, at].reshape(rows, size)
            q = q16.astype(F32)
            k = k_all[here, :, at].reshape(rows, size).astype(F32)
            v = v_all[here, :, at].reshape(rows, size).astype(F32)
            decay = jnp.exp(jnp.full((rows, size), -slope[h], F32))
            read = jnp.zeros((rows, size), F32)
            for r in range(block):
                read = jnp.where(owner == r, dot(q16, states[i * block + r, h]), read)
            k_before = pltpu.roll(k, 1, 0)
            v_before = pltpu.roll(v, 1, 0)
            same = jnp.sum(q * k, -1, keepdims=True)
            cross = jnp.sum(q * k_before, -1, keepdims=True)
            out = jnp.where(second, decay * decay, decay) * read + same * v
            out = out + jnp.where(second, decay * cross * v_before, 0.0)
            out = out * lax.rsqrt(jnp.mean(out * out, -1, keepdims=True) + 1e-06)
            parts.append((out * gain[:, at]).astype(BF))
        normed.append(jnp.concatenate(parts, 1) if heads > 1 else parts[0])
    normed = jnp.concatenate(normed, 0) if blocks > 1 else normed[0]
    normed_ref[...] = normed
    project_columns(weight_loads, weight, normed, 1 - lax.axis_index("side"), other_ref)


def attention(slopes, queries, new_keys, new_values, head_states, gain, out_weight, groups):
    requests, tokens, width = queries.shape
    piece = out_weight.shape[1] // (2 * groups)
    rows = requests * tokens
    vec = pltpu.VMEM(queries.shape, BF)
    operands = (slopes, queries, new_keys, new_values, head_states, gain, out_weight)
    return pl.pallas_call(
        attention_kernel,
        in_specs=hbm_specs(7),
        out_specs=whole_vmem(3),
        out_shape=[
            in_vmem((groups, rows, piece), BF),
            in_vmem((rows, width), BF),
            in_vmem(head_states.shape, BF),
        ],
        scratch_shapes=[
            pltpu.SMEM(slopes.shape, F32), vec, vec, vec,
            pltpu.VMEM(gain.shape, F32),
            pltpu.VMEM(columns_shape(out_weight, groups), BF),
            pltpu.SemaphoreType.DMA((5,)),
            pltpu.SemaphoreType.DMA((requests,)),
            pltpu.SemaphoreType.DMA((groups,)),
        ],
        compiler_params=params(),
        name="attention",
    )(*[from_hbm(x) if x.size > 1 else x for x in operands])


def project_kernel(w_hbm, normed_ref, mine_ref, weight, weight_sem):
    loads = load_columns(w_hbm, weight, weight_sem, lax.axis_index("side"))
    for copy in loads:
        copy.start()
    normed = normed_ref[...]
    project_columns(loads, weight, normed, lax.axis_index("side"), mine_ref)


def project(out_weight, normed, groups):
    piece = out_weight.shape[1] // (2 * groups)
    return pl.pallas_call(
        project_kernel,
        in_specs=hbm_specs(1) + whole_vmem(1),
        out_specs=whole_vmem(1)[0],
        out_shape=in_vmem((groups, normed.shape[0], piece), F32),
        scratch_shapes=[
            pltpu.VMEM(columns_shape(out_weight, groups), BF),
            pltpu.SemaphoreType.DMA((groups,)),
        ],
        compiler_params=params(),
        cost_estimate=cost(10**8, 2 * 10**6),
        name="project",
    )(from_hbm(out_weight), normed)


def state_kernel(slope_ref, k_ref, v_ref, s_ref, after_ref, so_hbm, done_ref, out, sems):
    del after_ref
    done_ref[...] = jnp.zeros_like(done_ref)
    requests, tokens, _ = k_ref.shape
    heads, size = s_ref.shape[1], s_ref.shape[2]
    block = 8 if requests % 8 == 0 else requests
    rows = block * tokens
    row = lax.broadcasted_iota(jnp.int32, (rows, size), 0)
    second = row % tokens == 1
    owner = row // tokens
    stores = []
    for i in range(requests // block):
        here = slice(i * block, (i + 1) * block)
        for h in range(heads):
            at = slice(h * size, (h + 1) * size)
            k16 = k_ref[here, :, at].reshape(rows, size)
            v = v_ref[here, :, at].reshape(rows, size).astype(F32)
            decay = jnp.exp(jnp.full((rows, size), -slope_ref[h], F32))
            weighted = jnp.where(second, v, decay * v)
            spread = jnp.concatenate(
                [jnp.where(owner == r, weighted, 0.0).astype(BF) for r in range(block)], 1
            )
            update = lax.dot_general(
                k16, spread, (((0,), (0,)), ((), ())), preferred_element_type=F32
            )
            keep = jnp.exp(jnp.full((size, size), -2.0 * slope_ref[h], F32))
            for r in range(block):
                out[i * block + r, h] = (
                    keep * s_ref[i * block + r, h].astype(F32)
                    + update[:, r * size : (r + 1) * size]
                ).astype(BF)
        part = pl.ds(i * block, block)
        stores.append(pltpu.make_async_copy(out.at[part], so_hbm.at[part], sems.at[i]))
        stores[-1].start()
    for copy in stores:
        copy.wait()


def new_state(slopes, new_keys, new_values, head_states, after):
    return pl.pallas_call(
        state_kernel,
        in_specs=[
            pl.BlockSpec(memory_space=pltpu.SMEM), *whole_vmem(3),
            pl.BlockSpec(memory_space=pl.ANY),
        ],
        out_specs=[*hbm_specs(1), *whole_vmem(1)],
        out_shape=[struct(head_states.shape, BF), struct((8, 128), F32)],
        scratch_shapes=[
            pltpu.VMEM(head_states.shape, BF),
            pltpu.SemaphoreType.DMA((head_states.shape[0],)),
        ],
        compiler_params=params(),
        cost_estimate=cost(10**8, 8 * 10**6),
        name="new_state",
    )(slopes, new_keys, new_values, head_states, after)


def split_kernel(mine_ref, recv_ref, own_ref, *send_refs):
    me = lax.axis_index("heads")
    own_ref[...] = mine_ref[me].astype(F32) + recv_ref[me].astype(F32)
    for k, send_ref in zip(range(len(send_refs), 0, -1), send_refs):
        at = me ^ k
        send_ref[...] = (mine_ref[at].astype(F32) + recv_ref[at].astype(F32)).astype(BF)


def split(mine, recv):
    groups, rows, piece = mine.shape
    return pl.pallas_call(
        split_kernel,
        in_specs=whole_vmem(2),
        out_specs=whole_vmem(groups),
        out_shape=[struct((rows, piece), F32)] + [struct((rows, piece), BF)] * (groups - 1),
        compiler_params=params(),
        name="split_sum",
    )(mine, recv)


def residual_kernel(residual_ref, after_ref, own_ref, *refs):
    del after_ref
    recv_refs, flat_ref = refs[:-1], refs[-1]
    total = own_ref[...]
    for recv_ref in recv_refs:
        total = total + recv_ref[...].astype(F32)
    total = residual_ref[...].astype(F32).reshape(total.shape) + total
    flat_ref[...] = total.astype(BF)


def add_residual(residual, after, own, recvs):
    return pl.pallas_call(
        residual_kernel,
        in_specs=[whole_vmem(1)[0], pl.BlockSpec(memory_space=pl.ANY)] + whole_vmem(1 + len(recvs)),
        out_specs=pl.BlockSpec(memory_space=pltpu.VMEM),
        out_shape=struct(own.shape, BF),
        compiler_params=params(),
        name="add_residual",
    )(residual, after, own, *recvs)


def reshape_kernel(flat_ref, out_ref):
    out_ref[...] = flat_ref[...].reshape(out_ref.shape)


def by_request(flat, shape):
    return pl.pallas_call(
        reshape_kernel,
        in_specs=whole_vmem(1),
        out_specs=pl.BlockSpec(memory_space=pltpu.VMEM),
        out_shape=struct(shape, BF),
        compiler_params=params(),
        cost_estimate=cost(10**5, 10**6),
        name="by_request",
    )(flat)


def route_kernel(capacity, ids_ref, gates_ref, after_ref, pick_ref, high_ref, low_ref):
    del after_ref
    here = lax.axis_index("dp")
    tokens, choices, requests = ids_ref.shape
    rows, total = pick_ref.shape
    row = lax.broadcasted_iota(jnp.int32, (rows, requests), 0)
    lane = lax.broadcasted_iota(jnp.int32, (rows, requests), 1)
    mine = [(row // tokens == lane) & (row % tokens == s) for s in range(tokens)]
    ids, gates = [], []
    for c in range(choices):
        number, gate = jnp.zeros((rows, requests), jnp.int32), jnp.zeros((rows, requests), F32)
        for s in range(tokens):
            number = number + jnp.where(mine[s], ids_ref[s, c : c + 1, :], 0)
            gate = gate + jnp.where(mine[s], gates_ref[s, c : c + 1, :], 0.0)
        ids.append(jnp.sum(number.astype(F32), -1, keepdims=True).astype(jnp.int32))
        gates.append(jnp.sum(gate, -1, keepdims=True))
    column = lax.broadcasted_iota(jnp.int32, (rows, total), 1)
    expert = here ^ (column // capacity)
    chosen, weight = jnp.zeros((rows, total), F32), jnp.zeros((rows, total), F32)
    for c in range(choices):
        named = ids[c] == expert
        chosen = jnp.where(named, 1.0, chosen)
        weight = jnp.where(named, gates[c], weight)
    earlier = lax.broadcasted_iota(jnp.int32, (rows, rows), 1) < lax.broadcasted_iota(
        jnp.int32, (rows, rows), 0
    )
    place = dot(jnp.where(earlier, 1.0, 0.0).astype(BF), chosen.astype(BF))
    hit = (chosen > 0.5) & (place.astype(jnp.int32) == column % capacity)
    pick_ref[...] = jnp.where(hit, 1.0, 0.0).astype(BF)
    weight = jnp.where(hit, weight, 0.0)
    high = weight.astype(BF)
    high_ref[...] = high
    low_ref[...] = (weight - high.astype(F32)).astype(BF)


def route(ids, gates, after, capacity, count):
    rows = ids.shape[0] * ids.shape[2]
    return pl.pallas_call(
        functools.partial(route_kernel, capacity),
        in_specs=whole_vmem(2) + [pl.BlockSpec(memory_space=pl.ANY)],
        out_specs=whole_vmem(3),
        out_shape=[struct((rows, count * capacity), BF)] * 3,
        compiler_params=params(),
        cost_estimate=cost(10**5, 10**6),
        name="route",
    )(ids, gates, after)


def dispatch_kernel(count, after_ref, pick_ref, *refs):
    del after_ref
    x_refs, out_refs = refs[:-count], refs[-count:]
    capacity = out_refs[0].shape[0] // len(x_refs)
    picked = [
        lax.dot_general(
            pick_ref[...], x_ref[...], (((0,), (0,)), ((), ())), preferred_element_type=F32
        )
        for x_ref in x_refs
    ]
    for k, out_ref in zip((0, *range(count - 1, 0, -1)), out_refs):
        rows = [x[k * capacity : (k + 1) * capacity] for x in picked]
        out_ref[...] = jnp.concatenate(rows, 0).astype(BF)


def dispatch(after, pick, xs, count):
    piece = xs[0].shape[1]
    rows = len(xs) * pick.shape[1] // count
    return pl.pallas_call(
        functools.partial(dispatch_kernel, count),
        in_specs=[pl.BlockSpec(memory_space=pl.ANY)] + whole_vmem(1 + len(xs)),
        out_specs=whole_vmem(count),
        out_shape=[struct((rows, piece), BF)] * count,
        compiler_params=params(),
        name="dispatch",
    )(after, pick, *xs)


def gate_up_kernel(gain_ref, wg_ref, wu_ref, *refs):
    x_refs, (out_ref, placed) = refs[:-2], refs[-2:]
    me, side = lax.axis_index("heads"), lax.axis_index("side")
    groups, total, piece = placed.shape
    hidden = wg_ref.shape[3]
    capacity = total // len(x_refs)
    squares = jnp.zeros((total, 1), F32)
    xs = [x_ref[...].astype(F32) for x_ref in x_refs]
    for k in range(groups):
        at = me ^ k
        x = jnp.concatenate([x[k * capacity : (k + 1) * capacity] for x in xs], 0)
        squares = squares + jnp.sum(x * x, -1, keepdims=True)
        placed[at] = x.astype(BF)
    parts = []
    for a in range(groups):
        low = gain_ref[:, 2 * a * piece : (2 * a + 1) * piece]
        high = gain_ref[:, (2 * a + 1) * piece : (2 * a + 2) * piece]
        gain = jnp.where(side == 0, low, high)
        parts.append((placed[a].astype(F32) * gain).astype(BF))
    lhs = jnp.concatenate(parts, 1)
    wide = 384 if hidden % 384 == 0 else hidden
    for n in range(0, hidden, wide):
        rhs = wg_ref[0, :, :, n : n + wide].reshape(groups * piece, wide)
        out_ref[:, n : n + wide] = dot(lhs, rhs).astype(BF)
    for n in range(0, hidden, wide):
        rhs = wu_ref[0, :, :, n : n + wide].reshape(groups * piece, wide)
        out_ref[:, hidden + n : hidden + n + wide] = dot(lhs, rhs).astype(BF)
    coarse = squares.astype(BF)
    fine = (squares - coarse.astype(F32)).astype(BF)
    lane = lax.broadcasted_iota(jnp.int32, (total, 128), 1)
    extra = jnp.where(lane == 0, coarse.astype(F32), jnp.where(lane == 1, fine.astype(F32), 0.0))
    out_ref[:, 2 * hidden :] = extra.astype(BF)


def gate_up(gain, w_gate, w_up, xs):
    _, groups, piece, hidden = w_gate.shape
    total = xs[0].shape[0] // groups * len(xs)
    return pl.pallas_call(
        gate_up_kernel,
        in_specs=whole_vmem(3 + len(xs)),
        out_specs=pl.BlockSpec(memory_space=pltpu.VMEM),
        out_shape=struct((total, 2 * hidden + 128), BF),
        scratch_shapes=[pltpu.VMEM((groups, total, piece), BF)],
        compiler_params=params(),
        name="gate_up",
    )(gain, w_gate, w_up, *xs)


def regroup_kernel(w_hbm, after_ref, out_ref, weight, sems):
    del after_ref
    count = weight.shape[0]
    parts = sems.shape[0]
    size = count // parts
    loads = [
        pltpu.make_async_copy(
            w_hbm.at[0, pl.ds(i * size, size)], weight.at[pl.ds(i * size, size)], sems.at[i]
        )
        for i in range(parts)
    ]
    for copy in loads:
        copy.start()
    step = 48 if size % 48 == 0 else 32 if size % 32 == 0 else size
    for i, copy in enumerate(loads):
        copy.wait()

        def one(j, carry, i=i):
            at = pl.ds(pl.multiple_of(i * size + j * step, 16), step)
            out_ref[:, at, :] = weight[at].swapaxes(0, 1)
            return carry

        lax.fori_loop(0, size // step, one, 0)


def regroup(w_down, after):
    _, hidden, groups, piece = w_down.shape
    parts = 4 if hidden % 64 == 0 else 1
    return pl.pallas_call(
        regroup_kernel,
        in_specs=[*hbm_specs(1), pl.BlockSpec(memory_space=pl.ANY)],
        out_specs=whole_vmem(1)[0],
        out_shape=in_vmem((groups, hidden, piece), BF),
        scratch_shapes=[
            pltpu.VMEM((hidden, groups, piece), BF),
            pltpu.SemaphoreType.DMA((parts,)),
        ],
        compiler_params=params(),
        cost_estimate=cost(10**8, 7 * 10**6),
        name="regroup_down",
    )(from_hbm(w_down), after)


def load_kernel(w_hbm, after_ref, out_ref, sem):
    del after_ref
    copy = pltpu.make_async_copy(w_hbm, out_ref, sem)
    copy.start()
    copy.wait()


def load(w, after):
    return pl.pallas_call(
        load_kernel,
        in_specs=[*hbm_specs(1), pl.BlockSpec(memory_space=pl.ANY)],
        out_specs=whole_vmem(1)[0],
        out_shape=in_vmem(w.shape, w.dtype),
        scratch_shapes=[pltpu.SemaphoreType.DMA],
        compiler_params=params(),
        cost_estimate=cost(10**6, 7 * 10**6),
        name="load_weight",
    )(from_hbm(w), after)


def down_kernel(width, part_ref, recv_ref, w_ref, *out_refs):
    groups, hidden, piece = w_ref.shape
    capacity = part_ref.shape[0] // len(out_refs)
    extra = part_ref[:, 2 * hidden :].astype(F32) + recv_ref[:, 2 * hidden :].astype(F32)
    squares = extra[:, 0:1] + extra[:, 1:2]
    scale = lax.rsqrt(squares / width + 1e-06)
    gate = (part_ref[:, :hidden].astype(F32) + recv_ref[:, :hidden].astype(F32)) * scale
    up = (
        part_ref[:, hidden : 2 * hidden].astype(F32) + recv_ref[:, hidden : 2 * hidden].astype(F32)
    ) * scale
    act = (gate / (1.0 + jnp.exp(-gate)) * up).astype(BF)
    outs = [dot(act, w_ref[a]) for a in range(groups)]
    for d, out_ref in zip((0, *range(len(out_refs) - 1, 0, -1)), out_refs):
        rows = [out[d * capacity : (d + 1) * capacity] for out in outs]
        out_ref[...] = jnp.concatenate(rows, 0).astype(BF)


def down(width, part, recv, weights, count):
    groups, hidden, piece = weights.shape
    rows = part.shape[0] // count * groups
    return pl.pallas_call(
        functools.partial(down_kernel, width),
        in_specs=whole_vmem(3),
        out_specs=whole_vmem(count),
        out_shape=[struct((rows, piece), BF)] * count,
        compiler_params=params(),
        name="down",
    )(part, recv, weights)


def combine_kernel(count, high_ref, low_ref, after_ref, *refs):
    del after_ref
    y_refs, out_refs, total = refs[:count], refs[count:-1], refs[-1]
    me = lax.axis_index("heads")
    groups = total.shape[0]
    capacity = y_refs[0].shape[0] // groups
    ys = [y_ref[...].astype(F32) for y_ref in y_refs]
    for a in range(groups):
        y = jnp.concatenate([y[a * capacity : (a + 1) * capacity] for y in ys], 0).astype(BF)
        total[a] = dot(high_ref[...], y) + dot(low_ref[...], y)
    for k, out_ref in zip((0, *range(groups - 1, 0, -1)), out_refs):
        out_ref[...] = total[me ^ k].astype(out_ref.dtype)


def combine(high, low, after, ys, groups):
    rows, piece = high.shape[0], ys[0].shape[1]
    return pl.pallas_call(
        functools.partial(combine_kernel, len(ys)),
        in_specs=whole_vmem(2) + [pl.BlockSpec(memory_space=pl.ANY)] + whole_vmem(len(ys)),
        out_specs=whole_vmem(groups),
        out_shape=[struct((rows, piece), F32)] + [struct((rows, piece), BF)] * (groups - 1),
        scratch_shapes=[pltpu.VMEM((groups, rows, piece), F32)],
        compiler_params=params(),
        name="combine",
    )(high, low, after, *ys)


def finish_kernel(own_ref, *refs):
    recv_refs, out_ref = refs[:-1], refs[-1]
    total = own_ref[...]
    for recv_ref in recv_refs:
        total = total + recv_ref[...].astype(F32)
    out_ref[...] = total.astype(BF).reshape(out_ref.shape)


def finish(own, recvs, shape):
    return pl.pallas_call(
        finish_kernel,
        in_specs=whole_vmem(1 + len(recvs)),
        out_specs=pl.BlockSpec(memory_space=pltpu.VMEM),
        out_shape=struct(shape, BF),
        compiler_params=params(),
        name="finish",
    )(own, *recvs)


def swap(x, axis, k):
    size = lax.axis_size(axis)
    return lax.ppermute(x, axis, [(i, i ^ k) for i in range(size)])


def swaps(sends, axis):
    return [swap(x, axis, k) for k, x in zip(range(len(sends), 0, -1), sends)]


def local(
    queries, new_keys, new_values, head_states, slopes, head_gain, out_weight, residual,
    norm_gain, expert_ids, expert_gates, w_gate, w_up, w_down,
):
    groups, count = lax.axis_size("heads"), lax.axis_size("dp")
    width = norm_gain.shape[0]
    other, normed, states = attention(
        slopes, queries, new_keys, new_values, head_states,
        head_gain.reshape(1, -1), out_weight, groups,
    )
    mine = project(out_weight, normed, groups)
    own, *sends = split(mine, swap(other, "side", 1))
    weights = regroup(w_down, own)
    flat = add_residual(residual, weights, own, swaps(sends, "heads"))
    resid_out = by_request(flat, residual.shape)
    capacity = max(2, 3 * expert_ids.shape[2] * flat.shape[0] // (2 * count))
    pick, high, low = route(
        jnp.transpose(expert_ids, (1, 2, 0)), jnp.transpose(expert_gates, (1, 2, 0)), flat,
        capacity, count,
    )
    w_gate = load(w_gate, flat)
    gathered = [flat] + swaps([flat] * (groups - 1), "heads")[::-1]
    own, *sends = dispatch(w_gate, pick, gathered, count)
    w_up = load(w_up, own)
    xs = [own] + swaps(sends, "dp")[::-1]
    part = gate_up(norm_gain.reshape(1, -1), w_gate, w_up, xs)
    own, *sends = down(width, part, swap(part, "side", 1), weights, count)
    state_out, done = new_state(slopes, new_keys, new_values, states, own)
    ys = [own] + swaps(sends, "dp")[::-1]
    own, *sends = combine(high, low, done, ys, groups)
    return state_out, resid_out, finish(own, swaps(sends, "heads"), residual.shape)


def solution(mesh):
    return jax.shard_map(
        local,
        mesh=mesh,
        in_specs=(
            P("dp", None, ("heads", "side")),
            P("dp", None, ("heads", "side")),
            P("dp", None, ("heads", "side")),
            P("dp", ("heads", "side"), None, None),
            P(("heads", "side")),
            P(("heads", "side")),
            P(("heads", "side"), None),
            P("dp", None, ("heads", "side")),
            P(),
            P("dp", None, None),
            P("dp", None, None),
            P("dp", None, "side", "heads"),
            P("dp", None, "side", "heads"),
            P("dp", "heads", None, "side"),
        ),
        out_specs=(
            P("dp", ("heads", "side"), None, None),
            P("dp", None, ("heads", "side")),
            P("dp", None, ("heads", "side")),
        ),
        check_vma=False,
    )
```

```python
import functools

import jax
import jax.numpy as jnp
from jax import lax
from jax.experimental import pallas as pl
from jax.experimental.pallas import tpu as pltpu
from jax.sharding import PartitionSpec as P

BF = jnp.bfloat16
F32 = jnp.float32
VMEM_LIMIT = 20 * 1024 * 1024
BIG_LIMIT = 58 * 1024 * 1024


def params(limit=VMEM_LIMIT):
    return pltpu.CompilerParams(vmem_limit_bytes=limit)


def struct(shape, dtype):
    return jax.ShapeDtypeStruct(shape, dtype)


def in_vmem(shape, dtype):
    return pltpu.VMEM(shape, dtype)


def from_hbm(x):
    return pltpu.with_memory_space_constraint(x, pltpu.HBM)


def hbm_specs(count):
    return [pl.BlockSpec(memory_space=pltpu.HBM)] * count


def whole_vmem(count):
    return [pl.BlockSpec(memory_space=pltpu.VMEM)] * count


def cost(flops, size):
    return pl.CostEstimate(flops=flops, bytes_accessed=size, transcendentals=0)


def dot(a, b):
    return jnp.dot(a, b, preferred_element_type=F32)


def load_columns(w_hbm, weight, sems, side):
    groups, _, piece = weight.shape
    if groups == 1:
        return [pltpu.make_async_copy(w_hbm, weight.at[0], sems.at[0])]
    return [
        pltpu.make_async_copy(
            w_hbm.at[:, pl.ds(pl.multiple_of((2 * a + side) * piece, 128), piece)],
            weight.at[a],
            sems.at[a],
        )
        for a in range(groups)
    ]


def columns_shape(out_weight, groups):
    rows, width = out_weight.shape
    piece = width // (2 * groups)
    return (groups, rows, piece) if piece % 128 == 0 else (1, rows, width)


def project_columns(loads, weight, normed, side, out_ref):
    groups, _, piece = out_ref.shape
    if weight.shape[0] == groups:
        for a in range(groups):
            if loads:
                loads[a].wait()
            out_ref[a] = dot(normed, weight[a]).astype(out_ref.dtype)
        return
    for copy in loads:
        copy.wait()
    for a in range(groups):
        both = dot(normed, weight[0, :, 2 * a * piece : 2 * (a + 1) * piece])
        out = jnp.where(side == 0, both[:, :piece], both[:, piece:])
        out_ref[a] = out.astype(out_ref.dtype)


def attention_kernel(
    slope_hbm, q_hbm, k_hbm, v_hbm, s_hbm, gain_hbm, w_hbm, other_ref, normed_ref, states, mine_weight,
    slope, q_all, k_all, v_all, gain, weight, small_sem, state_sem, weight_sem, mine_sem,
):
    small = [
        pltpu.make_async_copy(source, target, small_sem.at[i])
        for i, (source, target) in enumerate(
            ((q_hbm, q_all), (k_hbm, k_all), (v_hbm, v_all), (gain_hbm, gain), (slope_hbm, slope))
        )
    ]
    requests, tokens, _ = q_all.shape
    heads, size = states.shape[1], states.shape[2]
    block = 8 if requests % 8 == 0 else requests
    blocks = requests // block
    loads = [
        pltpu.make_async_copy(
            s_hbm.at[pl.ds(i * block, block)], states.at[pl.ds(i * block, block)], state_sem.at[i]
        )
        for i in range(blocks)
    ]
    side = lax.axis_index("side")
    weight_loads = load_columns(w_hbm, weight, weight_sem, 1 - side)
    mine_loads = load_columns(w_hbm, mine_weight, mine_sem, side)
    for copy in small + loads + weight_loads + mine_loads:
        copy.start()
    for copy in small:
        copy.wait()
    rows = block * tokens
    row = lax.broadcasted_iota(jnp.int32, (rows, size), 0)
    second = row % tokens == 1
    owner = row // tokens
    normed = []
    for i in range(blocks):
        loads[i].wait()
        parts = []
        for h in range(heads):
            at = slice(h * size, (h + 1) * size)
            here = slice(i * block, (i + 1) * block)
            q16 = q_all[here, :, at].reshape(rows, size)
            q = q16.astype(F32)
            k = k_all[here, :, at].reshape(rows, size).astype(F32)
            v = v_all[here, :, at].reshape(rows, size).astype(F32)
            decay = jnp.exp(jnp.full((rows, size), -slope[h], F32))
            side_by_side = [states[i * block + r, h] for r in range(block)]
            every = dot(q16, jnp.concatenate(side_by_side, 1))
            read = jnp.zeros((rows, size), F32)
            for r in range(block):
                read = jnp.where(owner == r, every[:, r * size : (r + 1) * size], read)
            k_before = pltpu.roll(k, 1, 0)
            v_before = pltpu.roll(v, 1, 0)
            same = jnp.sum(q * k, -1, keepdims=True)
            cross = jnp.sum(q * k_before, -1, keepdims=True)
            out = jnp.where(second, decay * decay, decay) * read + same * v
            out = out + jnp.where(second, decay * cross * v_before, 0.0)
            out = out * lax.rsqrt(jnp.mean(out * out, -1, keepdims=True) + 1e-06)
            parts.append((out * gain[:, at]).astype(BF))
        normed.append(jnp.concatenate(parts, 1) if heads > 1 else parts[0])
    normed = jnp.concatenate(normed, 0) if blocks > 1 else normed[0]
    normed_ref[...] = normed
    project_columns(weight_loads, weight, normed, 1 - side, other_ref)
    for copy in mine_loads:
        copy.wait()


def attention(slopes, queries, new_keys, new_values, head_states, gain, out_weight, groups):
    requests, tokens, width = queries.shape
    piece = out_weight.shape[1] // (2 * groups)
    rows = requests * tokens
    vec = pltpu.VMEM(queries.shape, BF)
    operands = (slopes, queries, new_keys, new_values, head_states, gain, out_weight)
    return pl.pallas_call(
        attention_kernel,
        in_specs=hbm_specs(7),
        out_specs=whole_vmem(4),
        out_shape=[
            in_vmem((groups, rows, piece), BF),
            in_vmem((rows, width), BF),
            in_vmem(head_states.shape, BF),
            in_vmem(columns_shape(out_weight, groups), BF),
        ],
        scratch_shapes=[
            pltpu.SMEM(slopes.shape, F32), vec, vec, vec,
            pltpu.VMEM(gain.shape, F32),
            pltpu.VMEM(columns_shape(out_weight, groups), BF),
            pltpu.SemaphoreType.DMA((5,)),
            pltpu.SemaphoreType.DMA((requests,)),
            pltpu.SemaphoreType.DMA((groups,)),
            pltpu.SemaphoreType.DMA((groups,)),
        ],
        compiler_params=params(),
        name="attention",
    )(*[from_hbm(x) if x.size > 1 else x for x in operands])


def project_kernel(normed_ref, weight, mine_ref):
    project_columns([], weight, normed_ref[...], lax.axis_index("side"), mine_ref)


def project(normed, weight, shape):
    return pl.pallas_call(
        project_kernel,
        in_specs=whole_vmem(2),
        out_specs=whole_vmem(1)[0],
        out_shape=in_vmem(shape, F32),
        compiler_params=params(),
        cost_estimate=cost(10**8, 2 * 10**6),
        name="project",
    )(normed, weight)


def state_kernel(slope_ref, k_ref, v_ref, s_ref, after_ref, so_hbm, done_ref, out, sems):
    del after_ref
    done_ref[...] = jnp.zeros_like(done_ref)
    requests, tokens, _ = k_ref.shape
    heads, size = s_ref.shape[1], s_ref.shape[2]
    block = 8 if requests % 8 == 0 else requests
    rows = block * tokens
    row = lax.broadcasted_iota(jnp.int32, (rows, size), 0)
    second = row % tokens == 1
    owner = row // tokens
    stores = []
    for i in range(requests // block):
        here = slice(i * block, (i + 1) * block)
        for h in range(heads):
            at = slice(h * size, (h + 1) * size)
            k16 = k_ref[here, :, at].reshape(rows, size)
            v = v_ref[here, :, at].reshape(rows, size).astype(F32)
            decay = jnp.exp(jnp.full((rows, size), -slope_ref[h], F32))
            weighted = jnp.where(second, v, decay * v)
            spread = jnp.concatenate(
                [jnp.where(owner == r, weighted, 0.0).astype(BF) for r in range(block)], 1
            )
            update = lax.dot_general(
                k16, spread, (((0,), (0,)), ((), ())), preferred_element_type=F32
            )
            keep = jnp.exp(jnp.full((size, size), -2.0 * slope_ref[h], F32))
            for r in range(block):
                out[i * block + r, h] = (
                    keep * s_ref[i * block + r, h].astype(F32)
                    + update[:, r * size : (r + 1) * size]
                ).astype(BF)
        part = pl.ds(i * block, block)
        stores.append(pltpu.make_async_copy(out.at[part], so_hbm.at[part], sems.at[i]))
        stores[-1].start()
    for copy in stores:
        copy.wait()


def new_state(slopes, new_keys, new_values, head_states, after):
    return pl.pallas_call(
        state_kernel,
        in_specs=[
            pl.BlockSpec(memory_space=pltpu.SMEM), *whole_vmem(3),
            pl.BlockSpec(memory_space=pl.ANY),
        ],
        out_specs=[*hbm_specs(1), *whole_vmem(1)],
        out_shape=[struct(head_states.shape, BF), struct((8, 128), F32)],
        scratch_shapes=[
            pltpu.VMEM(head_states.shape, BF),
            pltpu.SemaphoreType.DMA((head_states.shape[0],)),
        ],
        compiler_params=params(),
        cost_estimate=cost(10**8, 8 * 10**6),
        name="new_state",
    )(slopes, new_keys, new_values, head_states, after)


def split_kernel(mine_ref, recv_ref, own_ref, *send_refs):
    me = lax.axis_index("heads")
    own_ref[...] = mine_ref[me].astype(F32) + recv_ref[me].astype(F32)
    for k, send_ref in zip(range(len(send_refs), 0, -1), send_refs):
        at = me ^ k
        send_ref[...] = (mine_ref[at].astype(F32) + recv_ref[at].astype(F32)).astype(BF)


def split(mine, recv):
    groups, rows, piece = mine.shape
    return pl.pallas_call(
        split_kernel,
        in_specs=whole_vmem(2),
        out_specs=whole_vmem(groups),
        out_shape=[struct((rows, piece), F32)] + [struct((rows, piece), BF)] * (groups - 1),
        compiler_params=params(),
        name="split_sum",
    )(mine, recv)


def residual_kernel(residual_ref, after_ref, own_ref, *refs):
    del after_ref
    recv_refs, flat_ref = refs[:-1], refs[-1]
    total = own_ref[...]
    for recv_ref in recv_refs:
        total = total + recv_ref[...].astype(F32)
    total = residual_ref[...].astype(F32).reshape(total.shape) + total
    flat_ref[...] = total.astype(BF)


def add_residual(residual, after, own, recvs):
    return pl.pallas_call(
        residual_kernel,
        in_specs=[whole_vmem(1)[0], pl.BlockSpec(memory_space=pl.ANY)] + whole_vmem(1 + len(recvs)),
        out_specs=pl.BlockSpec(memory_space=pltpu.VMEM),
        out_shape=struct(own.shape, BF),
        compiler_params=params(),
        name="add_residual",
    )(residual, after, own, *recvs)


def reshape_kernel(flat_ref, out_ref):
    out_ref[...] = flat_ref[...].reshape(out_ref.shape)


def by_request(flat, shape):
    return pl.pallas_call(
        reshape_kernel,
        in_specs=whole_vmem(1),
        out_specs=pl.BlockSpec(memory_space=pltpu.VMEM),
        out_shape=struct(shape, BF),
        compiler_params=params(),
        cost_estimate=cost(10**5, 10**6),
        name="by_request",
    )(flat)


def route_kernel(capacity, ids_ref, gates_ref, after_ref, pick_ref, high_ref, low_ref):
    del after_ref
    here = lax.axis_index("dp")
    tokens, choices, requests = ids_ref.shape
    rows, total = pick_ref.shape
    row = lax.broadcasted_iota(jnp.int32, (rows, requests), 0)
    lane = lax.broadcasted_iota(jnp.int32, (rows, requests), 1)
    mine = [(row // tokens == lane) & (row % tokens == s) for s in range(tokens)]
    ids, gates = [], []
    for c in range(choices):
        number, gate = jnp.zeros((rows, requests), jnp.int32), jnp.zeros((rows, requests), F32)
        for s in range(tokens):
            number = number + jnp.where(mine[s], ids_ref[s, c : c + 1, :], 0)
            gate = gate + jnp.where(mine[s], gates_ref[s, c : c + 1, :], 0.0)
        ids.append(jnp.sum(number.astype(F32), -1, keepdims=True).astype(jnp.int32))
        gates.append(jnp.sum(gate, -1, keepdims=True))
    column = lax.broadcasted_iota(jnp.int32, (rows, total), 1)
    expert = here ^ (column // capacity)
    chosen, weight = jnp.zeros((rows, total), F32), jnp.zeros((rows, total), F32)
    for c in range(choices):
        named = ids[c] == expert
        chosen = jnp.where(named, 1.0, chosen)
        weight = jnp.where(named, gates[c], weight)
    earlier = lax.broadcasted_iota(jnp.int32, (rows, rows), 1) < lax.broadcasted_iota(
        jnp.int32, (rows, rows), 0
    )
    place = dot(jnp.where(earlier, 1.0, 0.0).astype(BF), chosen.astype(BF))
    hit = (chosen > 0.5) & (place.astype(jnp.int32) == column % capacity)
    pick_ref[...] = jnp.where(hit, 1.0, 0.0).astype(BF)
    weight = jnp.where(hit, weight, 0.0)
    high = weight.astype(BF)
    high_ref[...] = high
    low_ref[...] = (weight - high.astype(F32)).astype(BF)


def route(ids, gates, after, capacity, count):
    rows = ids.shape[0] * ids.shape[2]
    return pl.pallas_call(
        functools.partial(route_kernel, capacity),
        in_specs=whole_vmem(2) + [pl.BlockSpec(memory_space=pl.ANY)],
        out_specs=whole_vmem(3),
        out_shape=[struct((rows, count * capacity), BF)] * 3,
        compiler_params=params(),
        cost_estimate=cost(10**5, 10**6),
        name="route",
    )(ids, gates, after)


def dispatch_kernel(count, pick_ref, *refs):
    x_refs, out_refs = refs[:-count], refs[-count:]
    capacity = out_refs[0].shape[0] // len(x_refs)
    picked = [
        lax.dot_general(
            pick_ref[...], x_ref[...], (((0,), (0,)), ((), ())), preferred_element_type=F32
        )
        for x_ref in x_refs
    ]
    for k, out_ref in zip((0, *range(count - 1, 0, -1)), out_refs):
        rows = [x[k * capacity : (k + 1) * capacity] for x in picked]
        out_ref[...] = jnp.concatenate(rows, 0).astype(BF)


def dispatch(pick, xs, count):
    piece = xs[0].shape[1]
    rows = len(xs) * pick.shape[1] // count
    return pl.pallas_call(
        functools.partial(dispatch_kernel, count),
        in_specs=whole_vmem(1 + len(xs)),
        out_specs=whole_vmem(count),
        out_shape=[struct((rows, piece), BF)] * count,
        compiler_params=params(),
        name="dispatch",
    )(pick, *xs)


def products(lhs, wg_ref, wu_ref, start, stop, out_ref):
    _, groups, piece, _ = wg_ref.shape
    for i, w_ref in enumerate((wg_ref, wu_ref)):
        rhs = w_ref[0, :, :, start:stop].reshape(groups * piece, stop - start)
        at = i * (stop - start)
        out_ref[:, at : at + stop - start] = dot(lhs, rhs).astype(BF)


def first_kernel(split, gain_ref, wg_ref, wu_ref, *refs):
    x_refs, (out_ref, lhs_ref, placed) = refs[:-3], refs[-3:]
    me, side = lax.axis_index("heads"), lax.axis_index("side")
    groups, total, piece = placed.shape
    capacity = total // len(x_refs)
    squares = jnp.zeros((total, 1), F32)
    xs = [x_ref[...].astype(F32) for x_ref in (x_refs[0], *x_refs[:0:-1])]
    for k in range(groups):
        at = me ^ k
        x = jnp.concatenate([x[k * capacity : (k + 1) * capacity] for x in xs], 0)
        squares = squares + jnp.sum(x * x, -1, keepdims=True)
        placed[at] = x.astype(BF)
    parts = []
    for a in range(groups):
        low = gain_ref[:, 2 * a * piece : (2 * a + 1) * piece]
        high = gain_ref[:, (2 * a + 1) * piece : (2 * a + 2) * piece]
        gain = jnp.where(side == 0, low, high)
        parts.append((placed[a].astype(F32) * gain).astype(BF))
    lhs = jnp.concatenate(parts, 1)
    lhs_ref[...] = lhs
    products(lhs, wg_ref, wu_ref, 0, split, out_ref)
    coarse = squares.astype(BF)
    fine = (squares - coarse.astype(F32)).astype(BF)
    lane = lax.broadcasted_iota(jnp.int32, (total, 128), 1)
    extra = jnp.where(lane == 0, coarse.astype(F32), jnp.where(lane == 1, fine.astype(F32), 0.0))
    out_ref[:, 2 * split :] = extra.astype(BF)


def first_units(split, gain, w_gate, w_up, xs):
    _, groups, piece, _ = w_gate.shape
    total = xs[0].shape[0] // groups * len(xs)
    return pl.pallas_call(
        functools.partial(first_kernel, split),
        in_specs=whole_vmem(3 + len(xs)),
        out_specs=whole_vmem(2),
        out_shape=[
            in_vmem((total, 2 * split + 128), BF),
            in_vmem((total, groups * piece), BF),
        ],
        scratch_shapes=[pltpu.VMEM((groups, total, piece), BF)],
        compiler_params=params(),
        name="first_units",
    )(gain, w_gate, w_up, *xs)


def other_kernel(split, lhs_ref, wg_ref, wu_ref, out_ref):
    products(lhs_ref[...], wg_ref, wu_ref, split, wg_ref.shape[3], out_ref)


def other_units(split, lhs, w_gate, w_up):
    return pl.pallas_call(
        functools.partial(other_kernel, split),
        in_specs=whole_vmem(3),
        out_specs=whole_vmem(1)[0],
        out_shape=in_vmem((lhs.shape[0], 2 * (w_gate.shape[3] - split)), BF),
        compiler_params=params(),
        cost_estimate=cost(10**9, 4 * 10**6),
        name="other_units",
    )(lhs, w_gate, w_up)


def regroup_kernel(w_hbm, after_ref, out_ref, weight, sems):
    del after_ref
    count = weight.shape[0]
    parts = sems.shape[0]
    size = count // parts
    loads = [
        pltpu.make_async_copy(
            w_hbm.at[0, pl.ds(i * size, size)], weight.at[pl.ds(i * size, size)], sems.at[i]
        )
        for i in range(parts)
    ]
    for copy in loads:
        copy.start()
    step = 48 if size % 48 == 0 else 32 if size % 32 == 0 else size
    for i, copy in enumerate(loads):
        copy.wait()

        def one(j, carry, i=i):
            at = pl.ds(pl.multiple_of(i * size + j * step, 16), step)
            out_ref[:, at, :] = weight[at].swapaxes(0, 1)
            return carry

        lax.fori_loop(0, size // step, one, 0)


def regroup(w_down, after):
    _, hidden, groups, piece = w_down.shape
    parts = 4 if hidden % 64 == 0 else 1
    return pl.pallas_call(
        regroup_kernel,
        in_specs=[*hbm_specs(1), pl.BlockSpec(memory_space=pl.ANY)],
        out_specs=whole_vmem(1)[0],
        out_shape=in_vmem((groups, hidden, piece), BF),
        scratch_shapes=[
            pltpu.VMEM((hidden, groups, piece), BF),
            pltpu.SemaphoreType.DMA((parts,)),
        ],
        compiler_params=params(),
        cost_estimate=cost(10**8, 7 * 10**6),
        name="regroup_down",
    )(from_hbm(w_down), after)


def activation(part_ref, recv_ref, hidden, scale):
    gate = (part_ref[:, :hidden].astype(F32) + recv_ref[:, :hidden].astype(F32)) * scale
    up = (
        part_ref[:, hidden : 2 * hidden].astype(F32) + recv_ref[:, hidden : 2 * hidden].astype(F32)
    ) * scale
    return (gate / (1.0 + jnp.exp(-gate)) * up).astype(BF)


def down_first_kernel(width, split, part_ref, recv_ref, w_ref, sum_ref, scale_ref):
    extra = part_ref[:, 2 * split :].astype(F32) + recv_ref[:, 2 * split :].astype(F32)
    squares = extra[:, 0:1] + extra[:, 1:2]
    scale = lax.rsqrt(squares / width + 1e-06)
    scale_ref[...] = jnp.broadcast_to(scale, scale_ref.shape)
    act = activation(part_ref, recv_ref, split, scale)
    for a in range(w_ref.shape[0]):
        sum_ref[a] = dot(act, w_ref[a, :split])


def down_first(width, split, part, recv, weights):
    groups, _, piece = weights.shape
    total = part.shape[0]
    return pl.pallas_call(
        functools.partial(down_first_kernel, width, split),
        in_specs=whole_vmem(3),
        out_specs=whole_vmem(2),
        out_shape=[in_vmem((groups, total, piece), F32), in_vmem((total, 128), F32)],
        compiler_params=params(),
        cost_estimate=cost(10**9, 4 * 10**6),
        name="down_first",
    )(part, recv, weights)


def down_kernel(split, part_ref, recv_ref, w_ref, sum_ref, scale_ref, *out_refs):
    groups, hidden, _ = w_ref.shape
    capacity = part_ref.shape[0] // len(out_refs)
    act = activation(part_ref, recv_ref, hidden - split, scale_ref[:, 0:1])
    outs = [sum_ref[a] + dot(act, w_ref[a, split:]) for a in range(groups)]
    for d, out_ref in zip((0, *range(len(out_refs) - 1, 0, -1)), out_refs):
        rows = [out[d * capacity : (d + 1) * capacity] for out in outs]
        out_ref[...] = jnp.concatenate(rows, 0).astype(BF)


def down(split, part, recv, weights, sums, scale, count):
    groups, _, piece = weights.shape
    rows = part.shape[0] // count * groups
    return pl.pallas_call(
        functools.partial(down_kernel, split),
        in_specs=whole_vmem(5),
        out_specs=whole_vmem(count),
        out_shape=[in_vmem((rows, piece), BF)] * count,
        compiler_params=params(),
        name="down",
    )(part, recv, weights, sums, scale)


def combine_kernel(count, high_ref, low_ref, after_ref, *refs):
    del after_ref
    y_refs, out_refs, total = refs[:count], refs[count:-1], refs[-1]
    me = lax.axis_index("heads")
    groups = total.shape[0]
    capacity = y_refs[0].shape[0] // groups
    ys = [y_ref[...].astype(F32) for y_ref in y_refs]
    for a in range(groups):
        y = jnp.concatenate([y[a * capacity : (a + 1) * capacity] for y in ys], 0).astype(BF)
        total[a] = dot(high_ref[...], y) + dot(low_ref[...], y)
    for k, out_ref in zip((0, *range(groups - 1, 0, -1)), out_refs):
        out_ref[...] = total[me ^ k].astype(out_ref.dtype)


def combine(high, low, after, ys, groups):
    rows, piece = high.shape[0], ys[0].shape[1]
    return pl.pallas_call(
        functools.partial(combine_kernel, len(ys)),
        in_specs=whole_vmem(2) + [pl.BlockSpec(memory_space=pl.ANY)] + whole_vmem(len(ys)),
        out_specs=whole_vmem(groups),
        out_shape=[struct((rows, piece), F32)] + [struct((rows, piece), BF)] * (groups - 1),
        scratch_shapes=[pltpu.VMEM((groups, rows, piece), F32)],
        compiler_params=params(),
        name="combine",
    )(high, low, after, *ys)


def finish_kernel(own_ref, *refs):
    recv_refs, out_ref = refs[:-1], refs[-1]
    total = own_ref[...]
    for recv_ref in recv_refs:
        total = total + recv_ref[...].astype(F32)
    out_ref[...] = total.astype(BF).reshape(out_ref.shape)


def finish(own, recvs, shape):
    return pl.pallas_call(
        finish_kernel,
        in_specs=whole_vmem(1 + len(recvs)),
        out_specs=pl.BlockSpec(memory_space=pltpu.VMEM),
        out_shape=struct(shape, BF),
        compiler_params=params(),
        name="finish",
    )(own, *recvs)


def swap(x, axis, k):
    size = lax.axis_size(axis)
    return lax.ppermute(x, axis, [(i, i ^ k) for i in range(size)])


def swaps(sends, axis):
    return [swap(x, axis, k) for k, x in zip(range(len(sends), 0, -1), sends)]


def local(
    queries, new_keys, new_values, head_states, slopes, head_gain, out_weight, residual,
    norm_gain, expert_ids, expert_gates, w_gate, w_up, w_down,
):
    groups, count = lax.axis_size("heads"), lax.axis_size("dp")
    width = norm_gain.shape[0]
    other, normed, states, weight = attention(
        slopes, queries, new_keys, new_values, head_states,
        head_gain.reshape(1, -1), out_weight, groups,
    )
    mine = project(normed, weight, other.shape)
    own, *sends = split(mine, swap(other, "side", 1))
    weights = regroup(w_down, own)
    flat = add_residual(residual, weights, own, swaps(sends, "heads"))
    resid_out = by_request(flat, residual.shape)
    capacity = max(2, 3 * expert_ids.shape[2] * flat.shape[0] // (2 * count))
    pick, high, low = route(
        jnp.transpose(expert_ids, (1, 2, 0)), jnp.transpose(expert_gates, (1, 2, 0)), flat,
        capacity, count,
    )
    gathered = [flat] + swaps([flat] * (groups - 1), "heads")[::-1]
    own, *sends = dispatch(pick, gathered, count)
    xs = [own] + swaps(sends, "dp")
    hidden = w_gate.shape[3]
    split_at = hidden // 256 * 128
    part, lhs = first_units(split_at, norm_gain.reshape(1, -1), w_gate, w_up, xs)
    other_part = other_units(split_at, lhs, w_gate, w_up)
    sums, scale = down_first(width, split_at, part, swap(part, "side", 1), weights)
    own, *sends = down(
        split_at, other_part, swap(other_part, "side", 1), weights, sums, scale, count
    )
    state_out, done = new_state(slopes, new_keys, new_values, states, own)
    ys = [own] + swaps(sends, "dp")[::-1]
    own, *sends = combine(high, low, done, ys, groups)
    return state_out, resid_out, finish(own, swaps(sends, "heads"), residual.shape)


def solution(mesh):
    return jax.shard_map(
        local,
        mesh=mesh,
        in_specs=(
            P("dp", None, ("heads", "side")),
            P("dp", None, ("heads", "side")),
            P("dp", None, ("heads", "side")),
            P("dp", ("heads", "side"), None, None),
            P(("heads", "side")),
            P(("heads", "side")),
            P(("heads", "side"), None),
            P("dp", None, ("heads", "side")),
            P(),
            P("dp", None, None),
            P("dp", None, None),
            P("dp", None, "side", "heads"),
            P("dp", None, "side", "heads"),
            P("dp", "heads", None, "side"),
        ),
        out_specs=(
            P("dp", ("heads", "side"), None, None),
            P("dp", None, ("heads", "side")),
            P("dp", None, ("heads", "side")),
        ),
        check_vma=False,
    )
```

```python
import functools

import jax
import jax.numpy as jnp
from jax import lax
from jax.experimental import pallas as pl
from jax.experimental.pallas import tpu as pltpu
from jax.sharding import PartitionSpec as P

BF = jnp.bfloat16
F32 = jnp.float32
VMEM_LIMIT = 20 * 1024 * 1024
BIG_LIMIT = 58 * 1024 * 1024


def params(limit=VMEM_LIMIT):
    return pltpu.CompilerParams(vmem_limit_bytes=limit)


def struct(shape, dtype):
    return jax.ShapeDtypeStruct(shape, dtype)


def in_vmem(shape, dtype):
    return pltpu.VMEM(shape, dtype)


def from_hbm(x):
    return pltpu.with_memory_space_constraint(x, pltpu.HBM)


def hbm_specs(count):
    return [pl.BlockSpec(memory_space=pltpu.HBM)] * count


def whole_vmem(count):
    return [pl.BlockSpec(memory_space=pltpu.VMEM)] * count


def cost(flops, size):
    return pl.CostEstimate(flops=flops, bytes_accessed=size, transcendentals=0)


def dot(a, b):
    return jnp.dot(a, b, preferred_element_type=F32)


def side_of(a, mine):
    side = lax.axis_index("side")
    return jnp.where((lax.axis_index("heads") == a) == mine, side, 1 - side)


def load_columns(w_hbm, weight, sems, mine):
    groups, _, piece = weight.shape
    if groups == 1:
        return [pltpu.make_async_copy(w_hbm, weight.at[0], sems.at[0])]
    return [
        pltpu.make_async_copy(
            w_hbm.at[:, pl.ds(pl.multiple_of((2 * a + side_of(a, mine)) * piece, 128), piece)],
            weight.at[a],
            sems.at[a],
        )
        for a in range(groups)
    ]


def columns_shape(out_weight, groups):
    rows, width = out_weight.shape
    piece = width // (2 * groups)
    return (groups, rows, piece) if piece % 128 == 0 else (1, rows, width)


def project_columns(loads, weight, normed, mine, out_ref):
    groups, _, piece = out_ref.shape
    if weight.shape[0] == groups:
        for a in range(groups):
            if loads:
                loads[a].wait()
            out_ref[a] = dot(normed, weight[a]).astype(out_ref.dtype)
        return
    for copy in loads:
        copy.wait()
    for a in range(groups):
        both = dot(normed, weight[0, :, 2 * a * piece : 2 * (a + 1) * piece])
        out = jnp.where(side_of(a, mine) == 0, both[:, :piece], both[:, piece:])
        out_ref[a] = out.astype(out_ref.dtype)


def attention_kernel(
    slope_hbm, q_hbm, k_hbm, v_hbm, s_hbm, gain_hbm, w_hbm, other_ref, normed_ref, states, mine_weight,
    slope, q_all, k_all, v_all, gain, weight, small_sem, state_sem, weight_sem, mine_sem,
):
    small = [
        pltpu.make_async_copy(source, target, small_sem.at[i])
        for i, (source, target) in enumerate(
            ((q_hbm, q_all), (k_hbm, k_all), (v_hbm, v_all), (gain_hbm, gain), (slope_hbm, slope))
        )
    ]
    requests, tokens, _ = q_all.shape
    heads, size = states.shape[1], states.shape[2]
    block = 8 if requests % 8 == 0 else requests
    blocks = requests // block
    loads = [
        pltpu.make_async_copy(
            s_hbm.at[pl.ds(i * block, block)], states.at[pl.ds(i * block, block)], state_sem.at[i]
        )
        for i in range(blocks)
    ]
    weight_loads = load_columns(w_hbm, weight, weight_sem, False)
    mine_loads = load_columns(w_hbm, mine_weight, mine_sem, True)
    for copy in small + loads + weight_loads + mine_loads:
        copy.start()
    for copy in small:
        copy.wait()
    rows = block * tokens
    row = lax.broadcasted_iota(jnp.int32, (rows, size), 0)
    second = row % tokens == 1
    owner = row // tokens
    normed = []
    for i in range(blocks):
        loads[i].wait()
        parts = []
        for h in range(heads):
            at = slice(h * size, (h + 1) * size)
            here = slice(i * block, (i + 1) * block)
            q16 = q_all[here, :, at].reshape(rows, size)
            q = q16.astype(F32)
            k = k_all[here, :, at].reshape(rows, size).astype(F32)
            v = v_all[here, :, at].reshape(rows, size).astype(F32)
            decay = jnp.exp(jnp.full((rows, size), -slope[h], F32))
            side_by_side = [states[i * block + r, h] for r in range(block)]
            every = dot(q16, jnp.concatenate(side_by_side, 1))
            read = jnp.zeros((rows, size), F32)
            for r in range(block):
                read = jnp.where(owner == r, every[:, r * size : (r + 1) * size], read)
            k_before = pltpu.roll(k, 1, 0)
            v_before = pltpu.roll(v, 1, 0)
            same = jnp.sum(q * k, -1, keepdims=True)
            cross = jnp.sum(q * k_before, -1, keepdims=True)
            out = jnp.where(second, decay * decay, decay) * read + same * v
            out = out + jnp.where(second, decay * cross * v_before, 0.0)
            out = out * lax.rsqrt(jnp.mean(out * out, -1, keepdims=True) + 1e-06)
            parts.append((out * gain[:, at]).astype(BF))
        normed.append(jnp.concatenate(parts, 1) if heads > 1 else parts[0])
    normed = jnp.concatenate(normed, 0) if blocks > 1 else normed[0]
    normed_ref[...] = normed
    project_columns(weight_loads, weight, normed, False, other_ref)
    for copy in mine_loads:
        copy.wait()


def attention(slopes, queries, new_keys, new_values, head_states, gain, out_weight, groups):
    requests, tokens, width = queries.shape
    piece = out_weight.shape[1] // (2 * groups)
    rows = requests * tokens
    vec = pltpu.VMEM(queries.shape, BF)
    operands = (slopes, queries, new_keys, new_values, head_states, gain, out_weight)
    return pl.pallas_call(
        attention_kernel,
        in_specs=hbm_specs(7),
        out_specs=whole_vmem(4),
        out_shape=[
            in_vmem((groups, rows, piece), BF),
            in_vmem((rows, width), BF),
            in_vmem(head_states.shape, BF),
            in_vmem(columns_shape(out_weight, groups), BF),
        ],
        scratch_shapes=[
            pltpu.SMEM(slopes.shape, F32), vec, vec, vec,
            pltpu.VMEM(gain.shape, F32),
            pltpu.VMEM(columns_shape(out_weight, groups), BF),
            pltpu.SemaphoreType.DMA((5,)),
            pltpu.SemaphoreType.DMA((requests,)),
            pltpu.SemaphoreType.DMA((groups,)),
            pltpu.SemaphoreType.DMA((groups,)),
        ],
        compiler_params=params(),
        name="attention",
    )(*[from_hbm(x) if x.size > 1 else x for x in operands])


def project_kernel(normed_ref, weight, mine_ref):
    project_columns([], weight, normed_ref[...], True, mine_ref)


def project(normed, weight, shape):
    return pl.pallas_call(
        project_kernel,
        in_specs=whole_vmem(2),
        out_specs=whole_vmem(1)[0],
        out_shape=in_vmem(shape, F32),
        compiler_params=params(),
        cost_estimate=cost(10**8, 2 * 10**6),
        name="project",
    )(normed, weight)


def state_kernel(slope_ref, k_ref, v_ref, s_ref, after_ref, so_hbm, done_ref, out, sems):
    del after_ref
    done_ref[...] = jnp.zeros_like(done_ref)
    requests, tokens, _ = k_ref.shape
    heads, size = s_ref.shape[1], s_ref.shape[2]
    block = 8 if requests % 8 == 0 else requests
    rows = block * tokens
    row = lax.broadcasted_iota(jnp.int32, (rows, size), 0)
    second = row % tokens == 1
    owner = row // tokens
    stores = []
    for i in range(requests // block):
        here = slice(i * block, (i + 1) * block)
        for h in range(heads):
            at = slice(h * size, (h + 1) * size)
            k16 = k_ref[here, :, at].reshape(rows, size)
            v = v_ref[here, :, at].reshape(rows, size).astype(F32)
            decay = jnp.exp(jnp.full((rows, size), -slope_ref[h], F32))
            weighted = jnp.where(second, v, decay * v)
            spread = jnp.concatenate(
                [jnp.where(owner == r, weighted, 0.0).astype(BF) for r in range(block)], 1
            )
            update = lax.dot_general(
                k16, spread, (((0,), (0,)), ((), ())), preferred_element_type=F32
            )
            keep = jnp.exp(jnp.full((size, size), -2.0 * slope_ref[h], F32))
            for r in range(block):
                out[i * block + r, h] = (
                    keep * s_ref[i * block + r, h].astype(F32)
                    + update[:, r * size : (r + 1) * size]
                ).astype(BF)
        part = pl.ds(i * block, block)
        stores.append(pltpu.make_async_copy(out.at[part], so_hbm.at[part], sems.at[i]))
        stores[-1].start()
    for copy in stores:
        copy.wait()


def new_state(slopes, new_keys, new_values, head_states, after):
    return pl.pallas_call(
        state_kernel,
        in_specs=[
            pl.BlockSpec(memory_space=pltpu.SMEM), *whole_vmem(3),
            pl.BlockSpec(memory_space=pl.ANY),
        ],
        out_specs=[*hbm_specs(1), *whole_vmem(1)],
        out_shape=[struct(head_states.shape, BF), struct((8, 128), F32)],
        scratch_shapes=[
            pltpu.VMEM(head_states.shape, BF),
            pltpu.SemaphoreType.DMA((head_states.shape[0],)),
        ],
        compiler_params=params(),
        cost_estimate=cost(10**8, 8 * 10**6),
        name="new_state",
    )(slopes, new_keys, new_values, head_states, after)


def split_kernel(mine_ref, recv_ref, own_ref, *send_refs):
    me = lax.axis_index("heads")
    own_ref[...] = mine_ref[me].astype(F32) + recv_ref[me].astype(F32)
    for k, send_ref in zip(range(len(send_refs), 0, -1), send_refs):
        at = me ^ k
        send_ref[...] = (mine_ref[at].astype(F32) + recv_ref[at].astype(F32)).astype(BF)


def split(mine, recv):
    groups, rows, piece = mine.shape
    return pl.pallas_call(
        split_kernel,
        in_specs=whole_vmem(2),
        out_specs=whole_vmem(groups),
        out_shape=[struct((rows, piece), F32)] + [struct((rows, piece), BF)] * (groups - 1),
        compiler_params=params(),
        name="split_sum",
    )(mine, recv)


def residual_kernel(residual_ref, after_ref, own_ref, *refs):
    del after_ref
    count = (len(refs) - 1) // 2
    recv_refs, flat_refs = refs[:count], refs[count:]
    total = own_ref[...]
    for recv_ref in recv_refs:
        total = total + recv_ref[...].astype(F32)
    total = residual_ref[...].astype(F32).reshape(total.shape) + total
    for flat_ref in flat_refs:
        flat_ref[...] = total.astype(BF)


def add_residual(residual, after, own, recvs):
    return pl.pallas_call(
        residual_kernel,
        in_specs=[whole_vmem(1)[0], pl.BlockSpec(memory_space=pl.ANY)] + whole_vmem(1 + len(recvs)),
        out_specs=whole_vmem(1 + len(recvs)),
        out_shape=[in_vmem(own.shape, BF)] * (1 + len(recvs)),
        compiler_params=params(),
        name="add_residual",
    )(residual, after, own, *recvs)


def reshape_kernel(flat_ref, out_ref):
    out_ref[...] = flat_ref[...].reshape(out_ref.shape)


def by_request(flat, shape):
    return pl.pallas_call(
        reshape_kernel,
        in_specs=whole_vmem(1),
        out_specs=pl.BlockSpec(memory_space=pltpu.VMEM),
        out_shape=struct(shape, BF),
        compiler_params=params(),
        cost_estimate=cost(10**5, 10**6),
        name="by_request",
    )(flat)


def route_kernel(capacity, ids_ref, gates_ref, after_ref, pick_ref, high_ref, low_ref):
    del after_ref
    here = lax.axis_index("dp")
    tokens, choices, requests = ids_ref.shape
    rows, total = pick_ref.shape
    row = lax.broadcasted_iota(jnp.int32, (rows, requests), 0)
    lane = lax.broadcasted_iota(jnp.int32, (rows, requests), 1)
    mine = [(row // tokens == lane) & (row % tokens == s) for s in range(tokens)]
    ids, gates = [], []
    for c in range(choices):
        number, gate = jnp.zeros((rows, requests), jnp.int32), jnp.zeros((rows, requests), F32)
        for s in range(tokens):
            number = number + jnp.where(mine[s], ids_ref[s, c : c + 1, :], 0)
            gate = gate + jnp.where(mine[s], gates_ref[s, c : c + 1, :], 0.0)
        ids.append(jnp.sum(number.astype(F32), -1, keepdims=True).astype(jnp.int32))
        gates.append(jnp.sum(gate, -1, keepdims=True))
    column = lax.broadcasted_iota(jnp.int32, (rows, total), 1)
    expert = here ^ (column // capacity)
    chosen, weight = jnp.zeros((rows, total), F32), jnp.zeros((rows, total), F32)
    for c in range(choices):
        named = ids[c] == expert
        chosen = jnp.where(named, 1.0, chosen)
        weight = jnp.where(named, gates[c], weight)
    earlier = lax.broadcasted_iota(jnp.int32, (rows, rows), 1) < lax.broadcasted_iota(
        jnp.int32, (rows, rows), 0
    )
    place = dot(jnp.where(earlier, 1.0, 0.0).astype(BF), chosen.astype(BF))
    hit = (chosen > 0.5) & (place.astype(jnp.int32) == column % capacity)
    pick_ref[...] = jnp.where(hit, 1.0, 0.0).astype(BF)
    weight = jnp.where(hit, weight, 0.0)
    high = weight.astype(BF)
    high_ref[...] = high
    low_ref[...] = (weight - high.astype(F32)).astype(BF)


def route(ids, gates, after, capacity, count):
    rows = ids.shape[0] * ids.shape[2]
    return pl.pallas_call(
        functools.partial(route_kernel, capacity),
        in_specs=whole_vmem(2) + [pl.BlockSpec(memory_space=pl.ANY)],
        out_specs=whole_vmem(3),
        out_shape=[struct((rows, count * capacity), BF)] * 3,
        compiler_params=params(),
        cost_estimate=cost(10**5, 10**6),
        name="route",
    )(ids, gates, after)


def dispatch_kernel(count, pick_ref, *refs):
    x_refs, out_refs = refs[:-count], refs[-count:]
    capacity = out_refs[0].shape[0] // len(x_refs)
    picked = [
        lax.dot_general(
            pick_ref[...], x_ref[...], (((0,), (0,)), ((), ())), preferred_element_type=F32
        )
        for x_ref in x_refs
    ]
    for k, out_ref in zip((0, *range(count - 1, 0, -1)), out_refs):
        rows = [x[k * capacity : (k + 1) * capacity] for x in picked]
        out_ref[...] = jnp.concatenate(rows, 0).astype(BF)


def dispatch(pick, xs, count):
    piece = xs[0].shape[1]
    rows = len(xs) * pick.shape[1] // count
    return pl.pallas_call(
        functools.partial(dispatch_kernel, count),
        in_specs=whole_vmem(1 + len(xs)),
        out_specs=whole_vmem(count),
        out_shape=[struct((rows, piece), BF)] * count,
        compiler_params=params(),
        name="dispatch",
    )(pick, *xs)


def products(lhs, wg_ref, wu_ref, start, stop, out_ref):
    _, groups, piece, _ = wg_ref.shape
    for i, w_ref in enumerate((wg_ref, wu_ref)):
        rhs = w_ref[0, :, :, start:stop].reshape(groups * piece, stop - start)
        at = i * (stop - start)
        out_ref[:, at : at + stop - start] = dot(lhs, rhs).astype(BF)


def first_kernel(split, gain_ref, wg_ref, wu_ref, *refs):
    x_refs, (out_ref, lhs_ref, placed) = refs[:-3], refs[-3:]
    me, side = lax.axis_index("heads"), lax.axis_index("side")
    groups, total, piece = placed.shape
    capacity = total // len(x_refs)
    squares = jnp.zeros((total, 1), F32)
    xs = [x_ref[...].astype(F32) for x_ref in (x_refs[0], *x_refs[:0:-1])]
    for k in range(groups):
        at = me ^ ((groups - k) % groups)
        x = jnp.concatenate([x[k * capacity : (k + 1) * capacity] for x in xs], 0)
        squares = squares + jnp.sum(x * x, -1, keepdims=True)
        placed[at] = x.astype(BF)
    parts = []
    for a in range(groups):
        low = gain_ref[:, 2 * a * piece : (2 * a + 1) * piece]
        high = gain_ref[:, (2 * a + 1) * piece : (2 * a + 2) * piece]
        gain = jnp.where(side == 0, low, high)
        parts.append((placed[a].astype(F32) * gain).astype(BF))
    lhs = jnp.concatenate(parts, 1)
    lhs_ref[...] = lhs
    products(lhs, wg_ref, wu_ref, 0, split, out_ref)
    coarse = squares.astype(BF)
    fine = (squares - coarse.astype(F32)).astype(BF)
    lane = lax.broadcasted_iota(jnp.int32, (total, 128), 1)
    extra = jnp.where(lane == 0, coarse.astype(F32), jnp.where(lane == 1, fine.astype(F32), 0.0))
    out_ref[:, 2 * split :] = extra.astype(BF)


def first_units(split, gain, w_gate, w_up, xs):
    _, groups, piece, _ = w_gate.shape
    total = xs[0].shape[0] // groups * len(xs)
    return pl.pallas_call(
        functools.partial(first_kernel, split),
        in_specs=whole_vmem(3 + len(xs)),
        out_specs=whole_vmem(2),
        out_shape=[
            in_vmem((total, 2 * split + 128), BF),
            in_vmem((total, groups * piece), BF),
        ],
        scratch_shapes=[pltpu.VMEM((groups, total, piece), BF)],
        compiler_params=params(),
        name="first_units",
    )(gain, w_gate, w_up, *xs)


def other_kernel(split, lhs_ref, wg_ref, wu_ref, out_ref):
    products(lhs_ref[...], wg_ref, wu_ref, split, wg_ref.shape[3], out_ref)


def other_units(split, lhs, w_gate, w_up):
    return pl.pallas_call(
        functools.partial(other_kernel, split),
        in_specs=whole_vmem(3),
        out_specs=whole_vmem(1)[0],
        out_shape=in_vmem((lhs.shape[0], 2 * (w_gate.shape[3] - split)), BF),
        compiler_params=params(),
        cost_estimate=cost(10**9, 4 * 10**6),
        name="other_units",
    )(lhs, w_gate, w_up)


def regroup_kernel(w_hbm, after_ref, out_ref, weight, sems):
    del after_ref
    count = weight.shape[0]
    parts = sems.shape[0]
    size = count // parts
    loads = [
        pltpu.make_async_copy(
            w_hbm.at[0, pl.ds(i * size, size)], weight.at[pl.ds(i * size, size)], sems.at[i]
        )
        for i in range(parts)
    ]
    for copy in loads:
        copy.start()
    step = 48 if size % 48 == 0 else 32 if size % 32 == 0 else size
    for i, copy in enumerate(loads):
        copy.wait()

        def one(j, carry, i=i):
            at = pl.ds(pl.multiple_of(i * size + j * step, 16), step)
            out_ref[:, at, :] = weight[at].swapaxes(0, 1)
            return carry

        lax.fori_loop(0, size // step, one, 0)


def regroup(w_down, after):
    _, hidden, groups, piece = w_down.shape
    parts = 4 if hidden % 64 == 0 else 1
    return pl.pallas_call(
        regroup_kernel,
        in_specs=[*hbm_specs(1), pl.BlockSpec(memory_space=pl.ANY)],
        out_specs=whole_vmem(1)[0],
        out_shape=in_vmem((groups, hidden, piece), BF),
        scratch_shapes=[
            pltpu.VMEM((hidden, groups, piece), BF),
            pltpu.SemaphoreType.DMA((parts,)),
        ],
        compiler_params=params(),
        cost_estimate=cost(10**8, 7 * 10**6),
        name="regroup_down",
    )(from_hbm(w_down), after)


def activation(part_ref, recv_ref, hidden, scale):
    gate = (part_ref[:, :hidden].astype(F32) + recv_ref[:, :hidden].astype(F32)) * scale
    up = (
        part_ref[:, hidden : 2 * hidden].astype(F32) + recv_ref[:, hidden : 2 * hidden].astype(F32)
    ) * scale
    return (gate / (1.0 + jnp.exp(-gate)) * up).astype(BF)


def down_first_kernel(width, split, part_ref, recv_ref, w_ref, sum_ref, scale_ref):
    extra = part_ref[:, 2 * split :].astype(F32) + recv_ref[:, 2 * split :].astype(F32)
    squares = extra[:, 0:1] + extra[:, 1:2]
    scale = lax.rsqrt(squares / width + 1e-06)
    scale_ref[...] = jnp.broadcast_to(scale, scale_ref.shape)
    act = activation(part_ref, recv_ref, split, scale)
    for a in range(w_ref.shape[0]):
        sum_ref[a] = dot(act, w_ref[a, :split])


def down_first(width, split, part, recv, weights):
    groups, _, piece = weights.shape
    total = part.shape[0]
    return pl.pallas_call(
        functools.partial(down_first_kernel, width, split),
        in_specs=whole_vmem(3),
        out_specs=whole_vmem(2),
        out_shape=[in_vmem((groups, total, piece), F32), in_vmem((total, 128), F32)],
        compiler_params=params(),
        cost_estimate=cost(10**9, 4 * 10**6),
        name="down_first",
    )(part, recv, weights)


def down_kernel(split, part_ref, recv_ref, w_ref, sum_ref, scale_ref, *out_refs):
    groups, hidden, _ = w_ref.shape
    capacity = part_ref.shape[0] // len(out_refs)
    act = activation(part_ref, recv_ref, hidden - split, scale_ref[:, 0:1])
    outs = [sum_ref[a] + dot(act, w_ref[a, split:]) for a in range(groups)]
    for d, out_ref in zip((0, *range(len(out_refs) - 1, 0, -1)), out_refs):
        rows = [out[d * capacity : (d + 1) * capacity] for out in outs]
        out_ref[...] = jnp.concatenate(rows, 0).astype(BF)


def down(split, part, recv, weights, sums, scale, count):
    groups, _, piece = weights.shape
    rows = part.shape[0] // count * groups
    return pl.pallas_call(
        functools.partial(down_kernel, split),
        in_specs=whole_vmem(5),
        out_specs=whole_vmem(count),
        out_shape=[in_vmem((rows, piece), BF)] * count,
        compiler_params=params(),
        name="down",
    )(part, recv, weights, sums, scale)


def combine_kernel(count, high_ref, low_ref, after_ref, *refs):
    del after_ref
    y_refs, out_refs, total = refs[:count], refs[count:-1], refs[-1]
    me = lax.axis_index("heads")
    groups = total.shape[0]
    capacity = y_refs[0].shape[0] // groups
    ys = [y_ref[...].astype(F32) for y_ref in (y_refs[0], *y_refs[:0:-1])]
    for a in range(groups):
        y = jnp.concatenate([y[a * capacity : (a + 1) * capacity] for y in ys], 0).astype(BF)
        total[a] = dot(high_ref[...], y) + dot(low_ref[...], y)
    for k, out_ref in zip((0, *range(groups - 1, 0, -1)), out_refs):
        out_ref[...] = total[me ^ k].astype(out_ref.dtype)


def combine(high, low, after, ys, groups):
    rows, piece = high.shape[0], ys[0].shape[1]
    return pl.pallas_call(
        functools.partial(combine_kernel, len(ys)),
        in_specs=whole_vmem(2) + [pl.BlockSpec(memory_space=pl.ANY)] + whole_vmem(len(ys)),
        out_specs=whole_vmem(groups),
        out_shape=[struct((rows, piece), F32)] + [struct((rows, piece), BF)] * (groups - 1),
        scratch_shapes=[pltpu.VMEM((groups, rows, piece), F32)],
        compiler_params=params(),
        name="combine",
    )(high, low, after, *ys)


def finish_kernel(own_ref, *refs):
    recv_refs, out_ref = refs[:-1], refs[-1]
    total = own_ref[...]
    for recv_ref in recv_refs:
        total = total + recv_ref[...].astype(F32)
    out_ref[...] = total.astype(BF).reshape(out_ref.shape)


def finish(own, recvs, shape):
    return pl.pallas_call(
        finish_kernel,
        in_specs=whole_vmem(1 + len(recvs)),
        out_specs=pl.BlockSpec(memory_space=pltpu.VMEM),
        out_shape=struct(shape, BF),
        compiler_params=params(),
        name="finish",
    )(own, *recvs)


def swap(x, axis, k):
    size = lax.axis_size(axis)
    return lax.ppermute(x, axis, [(i, i ^ k) for i in range(size)])


def swaps(sends, axis):
    return [swap(x, axis, k) for k, x in zip(range(len(sends), 0, -1), sends)]


def cross_swaps(sends):
    size = lax.axis_size("heads")
    return [
        lax.ppermute(
            x, ("heads", "side"), [(2 * i + s, 2 * (i ^ k) + 1 - s) for i in range(size) for s in (0, 1)]
        )
        for k, x in zip(range(len(sends), 0, -1), sends)
    ]


def local(
    queries, new_keys, new_values, head_states, slopes, head_gain, out_weight, residual,
    norm_gain, expert_ids, expert_gates, w_gate, w_up, w_down,
):
    groups, count = lax.axis_size("heads"), lax.axis_size("dp")
    width = norm_gain.shape[0]
    other, normed, states, weight = attention(
        slopes, queries, new_keys, new_values, head_states,
        head_gain.reshape(1, -1), out_weight, groups,
    )
    mine = project(normed, weight, other.shape)
    own, *sends = split(mine, swap(other, "side", 1))
    weights = regroup(w_down, own)
    flat, *sends = add_residual(residual, weights, own, cross_swaps(sends))
    resid_out = by_request(flat, residual.shape)
    capacity = max(2, 3 * expert_ids.shape[2] * flat.shape[0] // (2 * count))
    pick, high, low = route(
        jnp.transpose(expert_ids, (1, 2, 0)), jnp.transpose(expert_gates, (1, 2, 0)), flat,
        capacity, count,
    )
    gathered = [flat] + swaps(sends, "heads")
    own, *sends = dispatch(pick, gathered, count)
    xs = [own] + swaps(sends, "dp")
    hidden = w_gate.shape[3]
    split_at = max(128, hidden // 384 * 256)
    part, lhs = first_units(split_at, norm_gain.reshape(1, -1), w_gate, w_up, xs)
    other_part = other_units(split_at, lhs, w_gate, w_up)
    sums, scale = down_first(width, split_at, part, swap(part, "side", 1), weights)
    own, *sends = down(
        split_at, other_part, swap(other_part, "side", 1), weights, sums, scale, count
    )
    state_out, done = new_state(slopes, new_keys, new_values, states, own)
    ys = [own] + swaps(sends, "dp")
    own, *sends = combine(high, low, done, ys, groups)
    return state_out, resid_out, finish(own, swaps(sends, "heads"), residual.shape)


def solution(mesh):
    return jax.shard_map(
        local,
        mesh=mesh,
        in_specs=(
            P("dp", None, ("heads", "side")),
            P("dp", None, ("heads", "side")),
            P("dp", None, ("heads", "side")),
            P("dp", ("heads", "side"), None, None),
            P(("heads", "side")),
            P(("heads", "side")),
            P(("heads", "side"), None),
            P("dp", None, ("heads", "side")),
            P(),
            P("dp", None, None),
            P("dp", None, None),
            P("dp", None, "side", "heads"),
            P("dp", None, "side", "heads"),
            P("dp", "heads", None, "side"),
        ),
        out_specs=(
            P("dp", ("heads", "side"), None, None),
            P("dp", None, ("heads", "side")),
            P("dp", None, ("heads", "side")),
        ),
        check_vma=False,
    )
```

```python
import functools

import jax
import jax.numpy as jnp
from jax import lax
from jax.experimental import pallas as pl
from jax.experimental.pallas import tpu as pltpu
from jax.sharding import PartitionSpec as P

BF = jnp.bfloat16
F32 = jnp.float32
VMEM_LIMIT = 20 * 1024 * 1024
BIG_LIMIT = 58 * 1024 * 1024


def params(limit=VMEM_LIMIT):
    return pltpu.CompilerParams(vmem_limit_bytes=limit)


def struct(shape, dtype):
    return jax.ShapeDtypeStruct(shape, dtype)


def in_vmem(shape, dtype):
    return pltpu.VMEM(shape, dtype)


def from_hbm(x):
    return pltpu.with_memory_space_constraint(x, pltpu.HBM)


def hbm_specs(count):
    return [pl.BlockSpec(memory_space=pltpu.HBM)] * count


def whole_vmem(count):
    return [pl.BlockSpec(memory_space=pltpu.VMEM)] * count


def cost(flops, size):
    return pl.CostEstimate(flops=flops, bytes_accessed=size, transcendentals=0)


def dot(a, b):
    return jnp.dot(a, b, preferred_element_type=F32)


def side_of(a, mine):
    side = lax.axis_index("side")
    return jnp.where((lax.axis_index("heads") == a) == mine, side, 1 - side)


def load_columns(w_hbm, weight, sems, mine):
    groups, _, piece = weight.shape
    if groups == 1:
        return [pltpu.make_async_copy(w_hbm, weight.at[0], sems.at[0])]
    return [
        pltpu.make_async_copy(
            w_hbm.at[:, pl.ds(pl.multiple_of((2 * a + side_of(a, mine)) * piece, 128), piece)],
            weight.at[a],
            sems.at[a],
        )
        for a in range(groups)
    ]


def columns_shape(out_weight, groups):
    rows, width = out_weight.shape
    piece = width // (2 * groups)
    return (groups, rows, piece) if piece % 128 == 0 else (1, rows, width)


def project_columns(loads, weight, normed, mine, out_ref):
    groups, _, piece = out_ref.shape
    if weight.shape[0] == groups:
        for a in range(groups):
            if loads:
                loads[a].wait()
            out_ref[a] = dot(normed, weight[a]).astype(out_ref.dtype)
        return
    for copy in loads:
        copy.wait()
    for a in range(groups):
        both = dot(normed, weight[0, :, 2 * a * piece : 2 * (a + 1) * piece])
        out = jnp.where(side_of(a, mine) == 0, both[:, :piece], both[:, piece:])
        out_ref[a] = out.astype(out_ref.dtype)


def attention_kernel(
    slope_hbm, q_hbm, k_hbm, v_hbm, s_hbm, gain_hbm, w_hbm, other_ref, normed_ref, states, mine_weight,
    slope, q_all, k_all, v_all, gain, weight, small_sem, state_sem, weight_sem, mine_sem,
):
    small = [
        pltpu.make_async_copy(source, target, small_sem.at[i])
        for i, (source, target) in enumerate(
            ((q_hbm, q_all), (k_hbm, k_all), (v_hbm, v_all), (gain_hbm, gain), (slope_hbm, slope))
        )
    ]
    requests, tokens, _ = q_all.shape
    heads, size = states.shape[1], states.shape[2]
    block = 8 if requests % 8 == 0 else requests
    blocks = requests // block
    loads = [
        pltpu.make_async_copy(
            s_hbm.at[pl.ds(i * block, block)], states.at[pl.ds(i * block, block)], state_sem.at[i]
        )
        for i in range(blocks)
    ]
    weight_loads = load_columns(w_hbm, weight, weight_sem, False)
    mine_loads = load_columns(w_hbm, mine_weight, mine_sem, True)
    for copy in small + loads + weight_loads + mine_loads:
        copy.start()
    for copy in small:
        copy.wait()
    rows = block * tokens
    row = lax.broadcasted_iota(jnp.int32, (rows, size), 0)
    second = row % tokens == 1
    owner = row // tokens
    normed = []
    for i in range(blocks):
        loads[i].wait()
        parts = []
        for h in range(heads):
            at = slice(h * size, (h + 1) * size)
            here = slice(i * block, (i + 1) * block)
            q16 = q_all[here, :, at].reshape(rows, size)
            q = q16.astype(F32)
            k = k_all[here, :, at].reshape(rows, size).astype(F32)
            v = v_all[here, :, at].reshape(rows, size).astype(F32)
            decay = jnp.exp(jnp.full((rows, size), -slope[h], F32))
            side_by_side = [states[i * block + r, h] for r in range(block)]
            every = dot(q16, jnp.concatenate(side_by_side, 1))
            read = jnp.zeros((rows, size), F32)
            for r in range(block):
                read = jnp.where(owner == r, every[:, r * size : (r + 1) * size], read)
            k_before = pltpu.roll(k, 1, 0)
            v_before = pltpu.roll(v, 1, 0)
            same = jnp.sum(q * k, -1, keepdims=True)
            cross = jnp.sum(q * k_before, -1, keepdims=True)
            out = jnp.where(second, decay * decay, decay) * read + same * v
            out = out + jnp.where(second, decay * cross * v_before, 0.0)
            out = out * lax.rsqrt(jnp.mean(out * out, -1, keepdims=True) + 1e-06)
            parts.append((out * gain[:, at]).astype(BF))
        normed.append(jnp.concatenate(parts, 1) if heads > 1 else parts[0])
    normed = jnp.concatenate(normed, 0) if blocks > 1 else normed[0]
    normed_ref[...] = normed
    project_columns(weight_loads, weight, normed, False, other_ref)
    for copy in mine_loads:
        copy.wait()


def attention(slopes, queries, new_keys, new_values, head_states, gain, out_weight, groups):
    requests, tokens, width = queries.shape
    piece = out_weight.shape[1] // (2 * groups)
    rows = requests * tokens
    vec = pltpu.VMEM(queries.shape, BF)
    operands = (slopes, queries, new_keys, new_values, head_states, gain, out_weight)
    return pl.pallas_call(
        attention_kernel,
        in_specs=hbm_specs(7),
        out_specs=whole_vmem(4),
        out_shape=[
            in_vmem((groups, rows, piece), BF),
            in_vmem((rows, width), BF),
            in_vmem(head_states.shape, BF),
            in_vmem(columns_shape(out_weight, groups), BF),
        ],
        scratch_shapes=[
            pltpu.SMEM(slopes.shape, F32), vec, vec, vec,
            pltpu.VMEM(gain.shape, F32),
            pltpu.VMEM(columns_shape(out_weight, groups), BF),
            pltpu.SemaphoreType.DMA((5,)),
            pltpu.SemaphoreType.DMA((requests,)),
            pltpu.SemaphoreType.DMA((groups,)),
            pltpu.SemaphoreType.DMA((groups,)),
        ],
        compiler_params=params(),
        name="attention",
    )(*[from_hbm(x) if x.size > 1 else x for x in operands])


def project_kernel(normed_ref, weight, mine_ref):
    project_columns([], weight, normed_ref[...], True, mine_ref)


def project(normed, weight, shape):
    return pl.pallas_call(
        project_kernel,
        in_specs=whole_vmem(2),
        out_specs=whole_vmem(1)[0],
        out_shape=in_vmem(shape, F32),
        compiler_params=params(),
        cost_estimate=cost(10**8, 2 * 10**6),
        name="project",
    )(normed, weight)


def state_kernel(slope_ref, k_ref, v_ref, s_ref, after_ref, so_hbm, done_ref, out, sems):
    del after_ref
    done_ref[...] = jnp.zeros_like(done_ref)
    requests, tokens, _ = k_ref.shape
    heads, size = s_ref.shape[1], s_ref.shape[2]
    block = 8 if requests % 8 == 0 else requests
    rows = block * tokens
    row = lax.broadcasted_iota(jnp.int32, (rows, size), 0)
    second = row % tokens == 1
    owner = row // tokens
    stores = []
    for i in range(requests // block):
        here = slice(i * block, (i + 1) * block)
        for h in range(heads):
            at = slice(h * size, (h + 1) * size)
            k16 = k_ref[here, :, at].reshape(rows, size)
            v = v_ref[here, :, at].reshape(rows, size).astype(F32)
            decay = jnp.exp(jnp.full((rows, size), -slope_ref[h], F32))
            weighted = jnp.where(second, v, decay * v)
            spread = jnp.concatenate(
                [jnp.where(owner == r, weighted, 0.0).astype(BF) for r in range(block)], 1
            )
            update = lax.dot_general(
                k16, spread, (((0,), (0,)), ((), ())), preferred_element_type=F32
            )
            keep = jnp.exp(jnp.full((size, size), -2.0 * slope_ref[h], F32))
            for r in range(block):
                out[i * block + r, h] = (
                    keep * s_ref[i * block + r, h].astype(F32)
                    + update[:, r * size : (r + 1) * size]
                ).astype(BF)
        part = pl.ds(i * block, block)
        stores.append(pltpu.make_async_copy(out.at[part], so_hbm.at[part], sems.at[i]))
        stores[-1].start()
    for copy in stores:
        copy.wait()


def new_state(slopes, new_keys, new_values, head_states, after):
    return pl.pallas_call(
        state_kernel,
        in_specs=[
            pl.BlockSpec(memory_space=pltpu.SMEM), *whole_vmem(3),
            pl.BlockSpec(memory_space=pl.ANY),
        ],
        out_specs=[*hbm_specs(1), *whole_vmem(1)],
        out_shape=[struct(head_states.shape, BF), struct((8, 128), F32)],
        scratch_shapes=[
            pltpu.VMEM(head_states.shape, BF),
            pltpu.SemaphoreType.DMA((head_states.shape[0],)),
        ],
        compiler_params=params(),
        cost_estimate=cost(10**8, 8 * 10**6),
        name="new_state",
    )(slopes, new_keys, new_values, head_states, after)


def split_kernel(mine_ref, recv_ref, own_ref, *send_refs):
    me = lax.axis_index("heads")
    own_ref[...] = mine_ref[me].astype(F32) + recv_ref[me].astype(F32)
    for k, send_ref in zip(range(len(send_refs), 0, -1), send_refs):
        at = me ^ k
        send_ref[...] = (mine_ref[at].astype(F32) + recv_ref[at].astype(F32)).astype(BF)


def split(mine, recv):
    groups, rows, piece = mine.shape
    return pl.pallas_call(
        split_kernel,
        in_specs=whole_vmem(2),
        out_specs=whole_vmem(groups),
        out_shape=[struct((rows, piece), F32)] + [struct((rows, piece), BF)] * (groups - 1),
        compiler_params=params(),
        name="split_sum",
    )(mine, recv)


def residual_kernel(residual_ref, after_ref, own_ref, *refs):
    del after_ref
    count = (len(refs) - 1) // 2
    recv_refs, flat_refs = refs[:count], refs[count:]
    total = own_ref[...]
    for recv_ref in recv_refs:
        total = total + recv_ref[...].astype(F32)
    total = residual_ref[...].astype(F32).reshape(total.shape) + total
    for flat_ref in flat_refs:
        flat_ref[...] = total.astype(BF)


def add_residual(residual, after, own, recvs):
    return pl.pallas_call(
        residual_kernel,
        in_specs=[whole_vmem(1)[0], pl.BlockSpec(memory_space=pl.ANY)] + whole_vmem(1 + len(recvs)),
        out_specs=whole_vmem(1 + len(recvs)),
        out_shape=[in_vmem(own.shape, BF)] * (1 + len(recvs)),
        compiler_params=params(),
        name="add_residual",
    )(residual, after, own, *recvs)


def reshape_kernel(flat_ref, out_ref):
    out_ref[...] = flat_ref[...].reshape(out_ref.shape)


def by_request(flat, shape):
    return pl.pallas_call(
        reshape_kernel,
        in_specs=whole_vmem(1),
        out_specs=pl.BlockSpec(memory_space=pltpu.VMEM),
        out_shape=struct(shape, BF),
        compiler_params=params(),
        cost_estimate=cost(10**5, 10**6),
        name="by_request",
    )(flat)


def route_kernel(capacity, ids_ref, gates_ref, after_ref, pick_ref, high_ref, low_ref):
    del after_ref
    here = lax.axis_index("dp")
    tokens, choices, requests = ids_ref.shape
    rows, total = pick_ref.shape
    row = lax.broadcasted_iota(jnp.int32, (rows, requests), 0)
    lane = lax.broadcasted_iota(jnp.int32, (rows, requests), 1)
    mine = [(row // tokens == lane) & (row % tokens == s) for s in range(tokens)]
    ids, gates = [], []
    for c in range(choices):
        number, gate = jnp.zeros((rows, requests), jnp.int32), jnp.zeros((rows, requests), F32)
        for s in range(tokens):
            number = number + jnp.where(mine[s], ids_ref[s, c : c + 1, :], 0)
            gate = gate + jnp.where(mine[s], gates_ref[s, c : c + 1, :], 0.0)
        ids.append(jnp.sum(number.astype(F32), -1, keepdims=True).astype(jnp.int32))
        gates.append(jnp.sum(gate, -1, keepdims=True))
    column = lax.broadcasted_iota(jnp.int32, (rows, total), 1)
    expert = here ^ (column // capacity)
    chosen, weight = jnp.zeros((rows, total), F32), jnp.zeros((rows, total), F32)
    for c in range(choices):
        named = ids[c] == expert
        chosen = jnp.where(named, 1.0, chosen)
        weight = jnp.where(named, gates[c], weight)
    earlier = lax.broadcasted_iota(jnp.int32, (rows, rows), 1) < lax.broadcasted_iota(
        jnp.int32, (rows, rows), 0
    )
    place = dot(jnp.where(earlier, 1.0, 0.0).astype(BF), chosen.astype(BF))
    hit = (chosen > 0.5) & (place.astype(jnp.int32) == column % capacity)
    pick_ref[...] = jnp.where(hit, 1.0, 0.0).astype(BF)
    weight = jnp.where(hit, weight, 0.0)
    high = weight.astype(BF)
    high_ref[...] = high
    low_ref[...] = (weight - high.astype(F32)).astype(BF)


def route(ids, gates, after, capacity, count):
    rows = ids.shape[0] * ids.shape[2]
    return pl.pallas_call(
        functools.partial(route_kernel, capacity),
        in_specs=whole_vmem(2) + [pl.BlockSpec(memory_space=pl.ANY)],
        out_specs=whole_vmem(3),
        out_shape=[struct((rows, count * capacity), BF)] * 3,
        compiler_params=params(),
        cost_estimate=cost(10**5, 10**6),
        name="route",
    )(ids, gates, after)


def dispatch_kernel(count, pick_ref, *refs):
    x_refs, out_refs = refs[:-count], refs[-count:]
    capacity = out_refs[0].shape[0] // len(x_refs)
    picked = [
        lax.dot_general(
            pick_ref[...], x_ref[...], (((0,), (0,)), ((), ())), preferred_element_type=F32
        )
        for x_ref in x_refs
    ]
    for k, out_ref in zip((0, *range(count - 1, 0, -1)), out_refs):
        rows = [x[k * capacity : (k + 1) * capacity] for x in picked]
        out_ref[...] = jnp.concatenate(rows, 0).astype(BF)


def dispatch(pick, xs, count):
    piece = xs[0].shape[1]
    rows = len(xs) * pick.shape[1] // count
    return pl.pallas_call(
        functools.partial(dispatch_kernel, count),
        in_specs=whole_vmem(1 + len(xs)),
        out_specs=whole_vmem(count),
        out_shape=[struct((rows, piece), BF)] * count,
        compiler_params=params(),
        name="dispatch",
    )(pick, *xs)


def products(lhs, wg_ref, wu_ref, start, stop, out_ref):
    _, groups, piece, _ = wg_ref.shape
    for i, w_ref in enumerate((wg_ref, wu_ref)):
        rhs = w_ref[0, :, :, start:stop].reshape(groups * piece, stop - start)
        at = i * (stop - start)
        out_ref[:, at : at + stop - start] = dot(lhs, rhs).astype(BF)


def first_kernel(split, gain_ref, wg_ref, wu_ref, *refs):
    x_refs, (out_ref, lhs_ref, placed) = refs[:-3], refs[-3:]
    me, side = lax.axis_index("heads"), lax.axis_index("side")
    groups, total, piece = placed.shape
    capacity = total // len(x_refs)
    squares = jnp.zeros((total, 1), F32)
    xs = [x_ref[...].astype(F32) for x_ref in (x_refs[0], *x_refs[:0:-1])]
    for k in range(groups):
        at = me ^ ((groups - k) % groups)
        x = jnp.concatenate([x[k * capacity : (k + 1) * capacity] for x in xs], 0)
        squares = squares + jnp.sum(x * x, -1, keepdims=True)
        placed[at] = x.astype(BF)
    parts = []
    for a in range(groups):
        low = gain_ref[:, 2 * a * piece : (2 * a + 1) * piece]
        high = gain_ref[:, (2 * a + 1) * piece : (2 * a + 2) * piece]
        gain = jnp.where(side == 0, low, high)
        parts.append((placed[a].astype(F32) * gain).astype(BF))
    lhs = jnp.concatenate(parts, 1)
    lhs_ref[...] = lhs
    products(lhs, wg_ref, wu_ref, 0, split, out_ref)
    coarse = squares.astype(BF)
    fine = (squares - coarse.astype(F32)).astype(BF)
    lane = lax.broadcasted_iota(jnp.int32, (total, 128), 1)
    extra = jnp.where(lane == 0, coarse.astype(F32), jnp.where(lane == 1, fine.astype(F32), 0.0))
    out_ref[:, 2 * split :] = extra.astype(BF)


def first_units(split, gain, w_gate, w_up, xs):
    _, groups, piece, _ = w_gate.shape
    total = xs[0].shape[0] // groups * len(xs)
    return pl.pallas_call(
        functools.partial(first_kernel, split),
        in_specs=whole_vmem(3 + len(xs)),
        out_specs=whole_vmem(2),
        out_shape=[
            in_vmem((total, 2 * split + 128), BF),
            in_vmem((total, groups * piece), BF),
        ],
        scratch_shapes=[pltpu.VMEM((groups, total, piece), BF)],
        compiler_params=params(),
        name="first_units",
    )(gain, w_gate, w_up, *xs)


def other_kernel(split, lhs_ref, wg_ref, wu_ref, out_ref):
    products(lhs_ref[...], wg_ref, wu_ref, split, wg_ref.shape[3], out_ref)


def other_units(split, lhs, w_gate, w_up):
    return pl.pallas_call(
        functools.partial(other_kernel, split),
        in_specs=whole_vmem(3),
        out_specs=whole_vmem(1)[0],
        out_shape=in_vmem((lhs.shape[0], 2 * (w_gate.shape[3] - split)), BF),
        compiler_params=params(),
        cost_estimate=cost(10**9, 4 * 10**6),
        name="other_units",
    )(lhs, w_gate, w_up)


def regroup_kernel(w_hbm, after_ref, out_ref, weight, sems):
    del after_ref
    count = weight.shape[0]
    parts = sems.shape[0]
    size = count // parts
    loads = [
        pltpu.make_async_copy(
            w_hbm.at[0, pl.ds(i * size, size)], weight.at[pl.ds(i * size, size)], sems.at[i]
        )
        for i in range(parts)
    ]
    for copy in loads:
        copy.start()
    step = 48 if size % 48 == 0 else 32 if size % 32 == 0 else size
    for i, copy in enumerate(loads):
        copy.wait()

        def one(j, carry, i=i):
            at = pl.ds(pl.multiple_of(i * size + j * step, 16), step)
            out_ref[:, at, :] = weight[at].swapaxes(0, 1)
            return carry

        lax.fori_loop(0, size // step, one, 0)


def regroup(w_down, after):
    _, hidden, groups, piece = w_down.shape
    parts = 4 if hidden % 64 == 0 else 1
    return pl.pallas_call(
        regroup_kernel,
        in_specs=[*hbm_specs(1), pl.BlockSpec(memory_space=pl.ANY)],
        out_specs=whole_vmem(1)[0],
        out_shape=in_vmem((groups, hidden, piece), BF),
        scratch_shapes=[
            pltpu.VMEM((hidden, groups, piece), BF),
            pltpu.SemaphoreType.DMA((parts,)),
        ],
        compiler_params=params(),
        cost_estimate=cost(10**8, 7 * 10**6),
        name="regroup_down",
    )(from_hbm(w_down), after)


def activation(part_ref, recv_ref, hidden, scale):
    gate = (part_ref[:, :hidden].astype(F32) + recv_ref[:, :hidden].astype(F32)) * scale
    up = (
        part_ref[:, hidden : 2 * hidden].astype(F32) + recv_ref[:, hidden : 2 * hidden].astype(F32)
    ) * scale
    return (gate / (1.0 + jnp.exp(-gate)) * up).astype(BF)


def down_first_kernel(width, split, part_ref, recv_ref, w_ref, sum_ref, scale_ref):
    extra = part_ref[:, 2 * split :].astype(F32) + recv_ref[:, 2 * split :].astype(F32)
    squares = extra[:, 0:1] + extra[:, 1:2]
    scale = lax.rsqrt(squares / width + 1e-06)
    scale_ref[...] = jnp.broadcast_to(scale, scale_ref.shape)
    act = activation(part_ref, recv_ref, split, scale)
    for a in range(w_ref.shape[0]):
        sum_ref[a] = dot(act, w_ref[a, :split])


def down_first(width, split, part, recv, weights):
    groups, _, piece = weights.shape
    total = part.shape[0]
    return pl.pallas_call(
        functools.partial(down_first_kernel, width, split),
        in_specs=whole_vmem(3),
        out_specs=whole_vmem(2),
        out_shape=[in_vmem((groups, total, piece), F32), in_vmem((total, 128), F32)],
        compiler_params=params(),
        cost_estimate=cost(10**9, 4 * 10**6),
        name="down_first",
    )(part, recv, weights)


def down_kernel(split, part_ref, recv_ref, w_ref, sum_ref, scale_ref, *out_refs):
    groups, hidden, _ = w_ref.shape
    capacity = part_ref.shape[0] // len(out_refs)
    act = activation(part_ref, recv_ref, hidden - split, scale_ref[:, 0:1])
    outs = [sum_ref[a] + dot(act, w_ref[a, split:]) for a in range(groups)]
    for d, out_ref in zip((0, *range(len(out_refs) - 1, 0, -1)), out_refs):
        rows = [out[d * capacity : (d + 1) * capacity] for out in outs]
        out_ref[...] = jnp.concatenate(rows, 0).astype(BF)


def down(split, part, recv, weights, sums, scale, count):
    groups, _, piece = weights.shape
    rows = part.shape[0] // count * groups
    return pl.pallas_call(
        functools.partial(down_kernel, split),
        in_specs=whole_vmem(5),
        out_specs=whole_vmem(count),
        out_shape=[in_vmem((rows, piece), BF)] * count,
        compiler_params=params(),
        name="down",
    )(part, recv, weights, sums, scale)


def combine_kernel(count, high_ref, low_ref, after_ref, *refs):
    del after_ref
    y_refs, out_refs, total = refs[:count], refs[count:-1], refs[-1]
    me = lax.axis_index("heads")
    groups = total.shape[0]
    capacity = y_refs[0].shape[0] // groups
    ys = [y_ref[...].astype(F32) for y_ref in (y_refs[0], *y_refs[:0:-1])]
    for a in range(groups):
        y = jnp.concatenate([y[a * capacity : (a + 1) * capacity] for y in ys], 0).astype(BF)
        total[a] = dot(high_ref[...], y) + dot(low_ref[...], y)
    for k, out_ref in zip((0, *range(groups - 1, 0, -1)), out_refs):
        out_ref[...] = total[me ^ k].astype(out_ref.dtype)


def combine(high, low, after, ys, groups):
    rows, piece = high.shape[0], ys[0].shape[1]
    return pl.pallas_call(
        functools.partial(combine_kernel, len(ys)),
        in_specs=whole_vmem(2) + [pl.BlockSpec(memory_space=pl.ANY)] + whole_vmem(len(ys)),
        out_specs=whole_vmem(groups),
        out_shape=[struct((rows, piece), F32)] + [struct((rows, piece), BF)] * (groups - 1),
        scratch_shapes=[pltpu.VMEM((groups, rows, piece), F32)],
        compiler_params=params(),
        name="combine",
    )(high, low, after, *ys)


def finish_kernel(own_ref, *refs):
    recv_refs, out_ref = refs[:-1], refs[-1]
    total = own_ref[...]
    for recv_ref in recv_refs:
        total = total + recv_ref[...].astype(F32)
    out_ref[...] = total.astype(BF).reshape(out_ref.shape)


def finish(own, recvs, shape):
    return pl.pallas_call(
        finish_kernel,
        in_specs=whole_vmem(1 + len(recvs)),
        out_specs=pl.BlockSpec(memory_space=pltpu.VMEM),
        out_shape=struct(shape, BF),
        compiler_params=params(),
        name="finish",
    )(own, *recvs)


def swap(x, axis, k):
    size = lax.axis_size(axis)
    return lax.ppermute(x, axis, [(i, i ^ k) for i in range(size)])


def swaps(sends, axis):
    return [swap(x, axis, k) for k, x in zip(range(len(sends), 0, -1), sends)]


def cross_swaps(sends):
    size = lax.axis_size("heads")
    return [
        lax.ppermute(
            x, ("heads", "side"), [(2 * i + s, 2 * (i ^ k) + 1 - s) for i in range(size) for s in (0, 1)]
        )
        for k, x in zip(range(len(sends), 0, -1), sends)
    ]


def local(
    queries, new_keys, new_values, head_states, slopes, head_gain, out_weight, residual,
    norm_gain, expert_ids, expert_gates, w_gate, w_up, w_down,
):
    groups, count = lax.axis_size("heads"), lax.axis_size("dp")
    width = norm_gain.shape[0]
    other, normed, states, weight = attention(
        slopes, queries, new_keys, new_values, head_states,
        head_gain.reshape(1, -1), out_weight, groups,
    )
    mine = project(normed, weight, other.shape)
    own, *sends = split(mine, swap(other, "side", 1))
    weights = regroup(w_down, own)
    flat, *sends = add_residual(residual, weights, own, cross_swaps(sends))
    resid_out = by_request(flat, residual.shape)
    capacity = max(2, 3 * expert_ids.shape[2] * flat.shape[0] // (2 * count))
    pick, high, low = route(
        jnp.transpose(expert_ids, (1, 2, 0)), jnp.transpose(expert_gates, (1, 2, 0)), flat,
        capacity, count,
    )
    gathered = [flat] + swaps(sends, "heads")
    own, *sends = dispatch(pick, gathered, count)
    xs = [own] + swaps(sends, "dp")
    hidden = w_gate.shape[3]
    split_at = (hidden + 128) // 256 * 128
    part, lhs = first_units(split_at, norm_gain.reshape(1, -1), w_gate, w_up, xs)
    other_part = other_units(split_at, lhs, w_gate, w_up)
    sums, scale = down_first(width, split_at, part, swap(part, "side", 1), weights)
    own, *sends = down(
        split_at, other_part, swap(other_part, "side", 1), weights, sums, scale, count
    )
    state_out, done = new_state(slopes, new_keys, new_values, states, own)
    ys = [own] + swaps(sends, "dp")
    own, *sends = combine(high, low, done, ys, groups)
    return state_out, resid_out, finish(own, swaps(sends, "heads"), residual.shape)


def solution(mesh):
    return jax.shard_map(
        local,
        mesh=mesh,
        in_specs=(
            P("dp", None, ("heads", "side")),
            P("dp", None, ("heads", "side")),
            P("dp", None, ("heads", "side")),
            P("dp", ("heads", "side"), None, None),
            P(("heads", "side")),
            P(("heads", "side")),
            P(("heads", "side"), None),
            P("dp", None, ("heads", "side")),
            P(),
            P("dp", None, None),
            P("dp", None, None),
            P("dp", None, "side", "heads"),
            P("dp", None, "side", "heads"),
            P("dp", "heads", None, "side"),
        ),
        out_specs=(
            P("dp", ("heads", "side"), None, None),
            P("dp", None, ("heads", "side")),
            P("dp", None, ("heads", "side")),
        ),
        check_vma=False,
    )
```

```python
import functools

import jax
import jax.numpy as jnp
from jax import lax
from jax.experimental import pallas as pl
from jax.experimental.pallas import tpu as pltpu
from jax.sharding import PartitionSpec as P

BF = jnp.bfloat16
F32 = jnp.float32
VMEM_LIMIT = 20 * 1024 * 1024
BIG_LIMIT = 58 * 1024 * 1024


def params(limit=VMEM_LIMIT):
    return pltpu.CompilerParams(vmem_limit_bytes=limit)


def struct(shape, dtype):
    return jax.ShapeDtypeStruct(shape, dtype)


def in_vmem(shape, dtype):
    return pltpu.VMEM(shape, dtype)


def from_hbm(x):
    return pltpu.with_memory_space_constraint(x, pltpu.HBM)


def hbm_specs(count):
    return [pl.BlockSpec(memory_space=pltpu.HBM)] * count


def whole_vmem(count):
    return [pl.BlockSpec(memory_space=pltpu.VMEM)] * count


def cost(flops, size):
    return pl.CostEstimate(flops=flops, bytes_accessed=size, transcendentals=0)


def dot(a, b):
    return jnp.dot(a, b, preferred_element_type=F32)


def side_of(a, mine):
    side = lax.axis_index("side")
    return jnp.where((lax.axis_index("heads") == a) == mine, side, 1 - side)


def load_columns(w_hbm, weight, sems, mine, first=0):
    groups, _, piece = weight.shape
    if piece == w_hbm.shape[1]:
        return [pltpu.make_async_copy(w_hbm, weight.at[0], sems.at[0])]
    return [
        pltpu.make_async_copy(
            w_hbm.at[:, pl.ds(pl.multiple_of((2 * a + side_of(a, mine)) * piece, 128), piece)],
            weight.at[a - first],
            sems.at[a],
        )
        for a in range(first, first + groups)
    ]


def columns_shape(out_weight, groups):
    rows, width = out_weight.shape
    piece = width // (2 * groups)
    return (groups, rows, piece) if piece % 128 == 0 else (1, rows, width)


def early_part(shape):
    return (shape[0] - shape[0] // 4, *shape[1:])


def project_columns(loads, weight, normed, mine, out_ref):
    groups, _, piece = out_ref.shape
    if weight.shape[0] == groups:
        for a in range(groups):
            if loads:
                loads[a].wait()
            out_ref[a] = dot(normed, weight[a]).astype(out_ref.dtype)
        return
    for copy in loads:
        copy.wait()
    for a in range(groups):
        both = dot(normed, weight[0, :, 2 * a * piece : 2 * (a + 1) * piece])
        out = jnp.where(side_of(a, mine) == 0, both[:, :piece], both[:, piece:])
        out_ref[a] = out.astype(out_ref.dtype)


def attention_kernel(
    slope_hbm, q_hbm, k_hbm, v_hbm, s_hbm, gain_hbm, w_hbm, other_ref, normed_ref, states, mine_weight,
    slope, q_all, k_all, v_all, gain, weight, small_sem, state_sem, weight_sem, mine_sem,
):
    small = [
        pltpu.make_async_copy(source, target, small_sem.at[i])
        for i, (source, target) in enumerate(
            ((q_hbm, q_all), (k_hbm, k_all), (v_hbm, v_all), (gain_hbm, gain), (slope_hbm, slope))
        )
    ]
    requests, tokens, _ = q_all.shape
    heads, size = states.shape[1], states.shape[2]
    block = 8 if requests % 8 == 0 else requests
    blocks = requests // block
    loads = [
        pltpu.make_async_copy(
            s_hbm.at[pl.ds(i * block, block)], states.at[pl.ds(i * block, block)], state_sem.at[i]
        )
        for i in range(blocks)
    ]
    weight_loads = load_columns(w_hbm, weight, weight_sem, False)
    mine_loads = load_columns(w_hbm, mine_weight, mine_sem, True)
    for copy in small + loads + weight_loads + mine_loads:
        copy.start()
    for copy in small:
        copy.wait()
    rows = block * tokens
    row = lax.broadcasted_iota(jnp.int32, (rows, size), 0)
    second = row % tokens == 1
    owner = row // tokens
    normed = []
    for i in range(blocks):
        loads[i].wait()
        parts = []
        for h in range(heads):
            at = slice(h * size, (h + 1) * size)
            here = slice(i * block, (i + 1) * block)
            q16 = q_all[here, :, at].reshape(rows, size)
            q = q16.astype(F32)
            k = k_all[here, :, at].reshape(rows, size).astype(F32)
            v = v_all[here, :, at].reshape(rows, size).astype(F32)
            decay = jnp.exp(jnp.full((rows, size), -slope[h], F32))
            side_by_side = [states[i * block + r, h] for r in range(block)]
            every = dot(q16, jnp.concatenate(side_by_side, 1))
            read = jnp.zeros((rows, size), F32)
            for r in range(block):
                read = jnp.where(owner == r, every[:, r * size : (r + 1) * size], read)
            k_before = pltpu.roll(k, 1, 0)
            v_before = pltpu.roll(v, 1, 0)
            same = jnp.sum(q * k, -1, keepdims=True)
            cross = jnp.sum(q * k_before, -1, keepdims=True)
            out = jnp.where(second, decay * decay, decay) * read + same * v
            out = out + jnp.where(second, decay * cross * v_before, 0.0)
            out = out * lax.rsqrt(jnp.mean(out * out, -1, keepdims=True) + 1e-06)
            parts.append((out * gain[:, at]).astype(BF))
        normed.append(jnp.concatenate(parts, 1) if heads > 1 else parts[0])
    normed = jnp.concatenate(normed, 0) if blocks > 1 else normed[0]
    normed_ref[...] = normed
    project_columns(weight_loads, weight, normed, False, other_ref)
    for copy in mine_loads:
        copy.wait()


def attention(slopes, queries, new_keys, new_values, head_states, gain, out_weight, groups):
    requests, tokens, width = queries.shape
    piece = out_weight.shape[1] // (2 * groups)
    rows = requests * tokens
    vec = pltpu.VMEM(queries.shape, BF)
    operands = (slopes, queries, new_keys, new_values, head_states, gain, out_weight)
    return pl.pallas_call(
        attention_kernel,
        in_specs=hbm_specs(7),
        out_specs=whole_vmem(4),
        out_shape=[
            in_vmem((groups, rows, piece), BF),
            in_vmem((rows, width), BF),
            in_vmem(head_states.shape, BF),
            in_vmem(early_part(columns_shape(out_weight, groups)), BF),
        ],
        scratch_shapes=[
            pltpu.SMEM(slopes.shape, F32), vec, vec, vec,
            pltpu.VMEM(gain.shape, F32),
            pltpu.VMEM(columns_shape(out_weight, groups), BF),
            pltpu.SemaphoreType.DMA((5,)),
            pltpu.SemaphoreType.DMA((requests,)),
            pltpu.SemaphoreType.DMA((groups,)),
            pltpu.SemaphoreType.DMA((groups,)),
        ],
        compiler_params=params(),
        name="attention",
    )(*[from_hbm(x) if x.size > 1 else x for x in operands])


def project_kernel(w_hbm, normed_ref, weight, mine_ref, later=None, sems=None):
    normed = normed_ref[...]
    if later is None:
        project_columns([], weight, normed, True, mine_ref)
        return
    held = weight.shape[0]
    loads = load_columns(w_hbm, later, sems, True, held)
    for copy in loads:
        copy.start()
    for a in range(held):
        mine_ref[a] = dot(normed, weight[a])
    for i, copy in enumerate(loads):
        copy.wait()
        mine_ref[held + i] = dot(normed, later[i])


def project(out_weight, normed, weight, shape):
    groups, held = shape[0], weight.shape[0]
    scratch = []
    if weight.shape[2] == shape[2] and held < groups:
        scratch = [
            pltpu.VMEM((groups - held, *weight.shape[1:]), BF),
            pltpu.SemaphoreType.DMA((groups,)),
        ]
    return pl.pallas_call(
        project_kernel,
        in_specs=hbm_specs(1) + whole_vmem(2),
        out_specs=whole_vmem(1)[0],
        out_shape=in_vmem(shape, F32),
        scratch_shapes=scratch,
        compiler_params=params(),
        cost_estimate=cost(10**8, 2 * 10**6),
        name="project",
    )(from_hbm(out_weight), normed, weight)


def state_kernel(slope_ref, k_ref, v_ref, s_ref, after_ref, so_hbm, done_ref, out, sems):
    del after_ref
    done_ref[...] = jnp.zeros_like(done_ref)
    requests, tokens, _ = k_ref.shape
    heads, size = s_ref.shape[1], s_ref.shape[2]
    block = 8 if requests % 8 == 0 else requests
    rows = block * tokens
    row = lax.broadcasted_iota(jnp.int32, (rows, size), 0)
    second = row % tokens == 1
    owner = row // tokens
    stores = []
    for i in range(requests // block):
        here = slice(i * block, (i + 1) * block)
        for h in range(heads):
            at = slice(h * size, (h + 1) * size)
            k16 = k_ref[here, :, at].reshape(rows, size)
            v = v_ref[here, :, at].reshape(rows, size).astype(F32)
            decay = jnp.exp(jnp.full((rows, size), -slope_ref[h], F32))
            weighted = jnp.where(second, v, decay * v)
            spread = jnp.concatenate(
                [jnp.where(owner == r, weighted, 0.0).astype(BF) for r in range(block)], 1
            )
            update = lax.dot_general(
                k16, spread, (((0,), (0,)), ((), ())), preferred_element_type=F32
            )
            keep = jnp.exp(jnp.full((size, size), -2.0 * slope_ref[h], F32))
            for r in range(block):
                out[i * block + r, h] = (
                    keep * s_ref[i * block + r, h].astype(F32)
                    + update[:, r * size : (r + 1) * size]
                ).astype(BF)
        part = pl.ds(i * block, block)
        stores.append(pltpu.make_async_copy(out.at[part], so_hbm.at[part], sems.at[i]))
        stores[-1].start()
    for copy in stores:
        copy.wait()


def new_state(slopes, new_keys, new_values, head_states, after):
    return pl.pallas_call(
        state_kernel,
        in_specs=[
            pl.BlockSpec(memory_space=pltpu.SMEM), *whole_vmem(3),
            pl.BlockSpec(memory_space=pl.ANY),
        ],
        out_specs=[*hbm_specs(1), *whole_vmem(1)],
        out_shape=[struct(head_states.shape, BF), struct((8, 128), F32)],
        scratch_shapes=[
            pltpu.VMEM(head_states.shape, BF),
            pltpu.SemaphoreType.DMA((head_states.shape[0],)),
        ],
        compiler_params=params(),
        cost_estimate=cost(10**8, 8 * 10**6),
        name="new_state",
    )(slopes, new_keys, new_values, head_states, after)


def split_kernel(mine_ref, recv_ref, own_ref, *send_refs):
    me = lax.axis_index("heads")
    own_ref[...] = mine_ref[me].astype(F32) + recv_ref[me].astype(F32)
    for k, send_ref in zip(range(len(send_refs), 0, -1), send_refs):
        at = me ^ k
        send_ref[...] = (mine_ref[at].astype(F32) + recv_ref[at].astype(F32)).astype(BF)


def split(mine, recv):
    groups, rows, piece = mine.shape
    return pl.pallas_call(
        split_kernel,
        in_specs=whole_vmem(2),
        out_specs=whole_vmem(groups),
        out_shape=[struct((rows, piece), F32)] + [struct((rows, piece), BF)] * (groups - 1),
        compiler_params=params(),
        name="split_sum",
    )(mine, recv)


def residual_kernel(residual_ref, after_ref, own_ref, *refs):
    del after_ref
    count = (len(refs) - 1) // 2
    recv_refs, flat_refs = refs[:count], refs[count:]
    total = own_ref[...]
    for recv_ref in recv_refs:
        total = total + recv_ref[...].astype(F32)
    total = residual_ref[...].astype(F32).reshape(total.shape) + total
    for flat_ref in flat_refs:
        flat_ref[...] = total.astype(BF)


def add_residual(residual, after, own, recvs):
    return pl.pallas_call(
        residual_kernel,
        in_specs=[whole_vmem(1)[0], pl.BlockSpec(memory_space=pl.ANY)] + whole_vmem(1 + len(recvs)),
        out_specs=whole_vmem(1 + len(recvs)),
        out_shape=[in_vmem(own.shape, BF)] * (1 + len(recvs)),
        compiler_params=params(),
        name="add_residual",
    )(residual, after, own, *recvs)


def reshape_kernel(flat_ref, out_ref):
    out_ref[...] = flat_ref[...].reshape(out_ref.shape)


def by_request(flat, shape):
    return pl.pallas_call(
        reshape_kernel,
        in_specs=whole_vmem(1),
        out_specs=pl.BlockSpec(memory_space=pltpu.VMEM),
        out_shape=struct(shape, BF),
        compiler_params=params(),
        cost_estimate=cost(10**5, 10**6),
        name="by_request",
    )(flat)


def route_kernel(capacity, ids_ref, gates_ref, after_ref, pick_ref, high_ref, low_ref):
    del after_ref
    here = lax.axis_index("dp")
    tokens, choices, requests = ids_ref.shape
    rows, total = pick_ref.shape
    row = lax.broadcasted_iota(jnp.int32, (rows, requests), 0)
    lane = lax.broadcasted_iota(jnp.int32, (rows, requests), 1)
    mine = [(row // tokens == lane) & (row % tokens == s) for s in range(tokens)]
    ids, gates = [], []
    for c in range(choices):
        number, gate = jnp.zeros((rows, requests), jnp.int32), jnp.zeros((rows, requests), F32)
        for s in range(tokens):
            number = number + jnp.where(mine[s], ids_ref[s, c : c + 1, :], 0)
            gate = gate + jnp.where(mine[s], gates_ref[s, c : c + 1, :], 0.0)
        ids.append(jnp.sum(number.astype(F32), -1, keepdims=True).astype(jnp.int32))
        gates.append(jnp.sum(gate, -1, keepdims=True))
    column = lax.broadcasted_iota(jnp.int32, (rows, total), 1)
    expert = here ^ (column // capacity)
    chosen, weight = jnp.zeros((rows, total), F32), jnp.zeros((rows, total), F32)
    for c in range(choices):
        named = ids[c] == expert
        chosen = jnp.where(named, 1.0, chosen)
        weight = jnp.where(named, gates[c], weight)
    earlier = lax.broadcasted_iota(jnp.int32, (rows, rows), 1) < lax.broadcasted_iota(
        jnp.int32, (rows, rows), 0
    )
    place = dot(jnp.where(earlier, 1.0, 0.0).astype(BF), chosen.astype(BF))
    hit = (chosen > 0.5) & (place.astype(jnp.int32) == column % capacity)
    pick_ref[...] = jnp.where(hit, 1.0, 0.0).astype(BF)
    weight = jnp.where(hit, weight, 0.0)
    high = weight.astype(BF)
    high_ref[...] = high
    low_ref[...] = (weight - high.astype(F32)).astype(BF)


def route(ids, gates, after, capacity, count):
    rows = ids.shape[0] * ids.shape[2]
    return pl.pallas_call(
        functools.partial(route_kernel, capacity),
        in_specs=whole_vmem(2) + [pl.BlockSpec(memory_space=pl.ANY)],
        out_specs=whole_vmem(3),
        out_shape=[struct((rows, count * capacity), BF)] * 3,
        compiler_params=params(),
        cost_estimate=cost(10**5, 10**6),
        name="route",
    )(ids, gates, after)


def dispatch_kernel(count, pick_ref, *refs):
    x_refs, out_refs = refs[:-count], refs[-count:]
    capacity = out_refs[0].shape[0] // len(x_refs)
    picked = [
        lax.dot_general(
            pick_ref[...], x_ref[...], (((0,), (0,)), ((), ())), preferred_element_type=F32
        )
        for x_ref in x_refs
    ]
    for k, out_ref in zip((0, *range(count - 1, 0, -1)), out_refs):
        rows = [x[k * capacity : (k + 1) * capacity] for x in picked]
        out_ref[...] = jnp.concatenate(rows, 0).astype(BF)


def dispatch(pick, xs, count):
    piece = xs[0].shape[1]
    rows = len(xs) * pick.shape[1] // count
    return pl.pallas_call(
        functools.partial(dispatch_kernel, count),
        in_specs=whole_vmem(1 + len(xs)),
        out_specs=whole_vmem(count),
        out_shape=[struct((rows, piece), BF)] * count,
        compiler_params=params(),
        name="dispatch",
    )(pick, *xs)


def products(lhs, wg_ref, wu_ref, start, stop, out_ref):
    _, groups, piece, _ = wg_ref.shape
    for i, w_ref in enumerate((wg_ref, wu_ref)):
        rhs = w_ref[0, :, :, start:stop].reshape(groups * piece, stop - start)
        at = i * (stop - start)
        out_ref[:, at : at + stop - start] = dot(lhs, rhs).astype(BF)


def first_kernel(split, gain_ref, wg_ref, wu_ref, *refs):
    x_refs, (out_ref, lhs_ref, placed) = refs[:-3], refs[-3:]
    me, side = lax.axis_index("heads"), lax.axis_index("side")
    groups, total, piece = placed.shape
    capacity = total // len(x_refs)
    squares = jnp.zeros((total, 1), F32)
    xs = [x_ref[...].astype(F32) for x_ref in (x_refs[0], *x_refs[:0:-1])]
    for k in range(groups):
        at = me ^ ((groups - k) % groups)
        x = jnp.concatenate([x[k * capacity : (k + 1) * capacity] for x in xs], 0)
        squares = squares + jnp.sum(x * x, -1, keepdims=True)
        placed[at] = x.astype(BF)
    parts = []
    for a in range(groups):
        low = gain_ref[:, 2 * a * piece : (2 * a + 1) * piece]
        high = gain_ref[:, (2 * a + 1) * piece : (2 * a + 2) * piece]
        gain = jnp.where(side == 0, low, high)
        parts.append((placed[a].astype(F32) * gain).astype(BF))
    lhs = jnp.concatenate(parts, 1)
    lhs_ref[...] = lhs
    products(lhs, wg_ref, wu_ref, 0, split, out_ref)
    coarse = squares.astype(BF)
    fine = (squares - coarse.astype(F32)).astype(BF)
    lane = lax.broadcasted_iota(jnp.int32, (total, 128), 1)
    extra = jnp.where(lane == 0, coarse.astype(F32), jnp.where(lane == 1, fine.astype(F32), 0.0))
    out_ref[:, 2 * split :] = extra.astype(BF)


def first_units(split, gain, w_gate, w_up, xs):
    _, groups, piece, _ = w_gate.shape
    total = xs[0].shape[0] // groups * len(xs)
    return pl.pallas_call(
        functools.partial(first_kernel, split),
        in_specs=whole_vmem(3 + len(xs)),
        out_specs=whole_vmem(2),
        out_shape=[
            in_vmem((total, 2 * split + 128), BF),
            in_vmem((total, groups * piece), BF),
        ],
        scratch_shapes=[pltpu.VMEM((groups, total, piece), BF)],
        compiler_params=params(),
        name="first_units",
    )(gain, w_gate, w_up, *xs)


def other_kernel(split, lhs_ref, wg_ref, wu_ref, out_ref):
    products(lhs_ref[...], wg_ref, wu_ref, split, wg_ref.shape[3], out_ref)


def other_units(split, lhs, w_gate, w_up):
    return pl.pallas_call(
        functools.partial(other_kernel, split),
        in_specs=whole_vmem(3),
        out_specs=whole_vmem(1)[0],
        out_shape=in_vmem((lhs.shape[0], 2 * (w_gate.shape[3] - split)), BF),
        compiler_params=params(),
        cost_estimate=cost(10**9, 4 * 10**6),
        name="other_units",
    )(lhs, w_gate, w_up)


def regroup_kernel(w_hbm, after_ref, out_ref, weight, sems):
    del after_ref
    count = weight.shape[0]
    parts = sems.shape[0]
    size = count // parts
    loads = [
        pltpu.make_async_copy(
            w_hbm.at[0, pl.ds(i * size, size)], weight.at[pl.ds(i * size, size)], sems.at[i]
        )
        for i in range(parts)
    ]
    for copy in loads:
        copy.start()
    step = 48 if size % 48 == 0 else 32 if size % 32 == 0 else size
    for i, copy in enumerate(loads):
        copy.wait()

        def one(j, carry, i=i):
            at = pl.ds(pl.multiple_of(i * size + j * step, 16), step)
            out_ref[:, at, :] = weight[at].swapaxes(0, 1)
            return carry

        lax.fori_loop(0, size // step, one, 0)


def regroup(w_down, after):
    _, hidden, groups, piece = w_down.shape
    parts = 4 if hidden % 64 == 0 else 1
    return pl.pallas_call(
        regroup_kernel,
        in_specs=[*hbm_specs(1), pl.BlockSpec(memory_space=pl.ANY)],
        out_specs=whole_vmem(1)[0],
        out_shape=in_vmem((groups, hidden, piece), BF),
        scratch_shapes=[
            pltpu.VMEM((hidden, groups, piece), BF),
            pltpu.SemaphoreType.DMA((parts,)),
        ],
        compiler_params=params(),
        cost_estimate=cost(10**8, 7 * 10**6),
        name="regroup_down",
    )(from_hbm(w_down), after)


def activation(part_ref, recv_ref, hidden, scale):
    gate = (part_ref[:, :hidden].astype(F32) + recv_ref[:, :hidden].astype(F32)) * scale
    up = (
        part_ref[:, hidden : 2 * hidden].astype(F32) + recv_ref[:, hidden : 2 * hidden].astype(F32)
    ) * scale
    return (gate / (1.0 + jnp.exp(-gate)) * up).astype(BF)


def down_first_kernel(width, split, part_ref, recv_ref, w_ref, sum_ref, scale_ref):
    extra = part_ref[:, 2 * split :].astype(F32) + recv_ref[:, 2 * split :].astype(F32)
    squares = extra[:, 0:1] + extra[:, 1:2]
    scale = lax.rsqrt(squares / width + 1e-06)
    scale_ref[...] = jnp.broadcast_to(scale, scale_ref.shape)
    act = activation(part_ref, recv_ref, split, scale)
    for a in range(w_ref.shape[0]):
        sum_ref[a] = dot(act, w_ref[a, :split])


def down_first(width, split, part, recv, weights):
    groups, _, piece = weights.shape
    total = part.shape[0]
    return pl.pallas_call(
        functools.partial(down_first_kernel, width, split),
        in_specs=whole_vmem(3),
        out_specs=whole_vmem(2),
        out_shape=[in_vmem((groups, total, piece), F32), in_vmem((total, 128), F32)],
        compiler_params=params(),
        cost_estimate=cost(10**9, 4 * 10**6),
        name="down_first",
    )(part, recv, weights)


def down_kernel(split, part_ref, recv_ref, w_ref, sum_ref, scale_ref, *out_refs):
    groups, hidden, _ = w_ref.shape
    capacity = part_ref.shape[0] // len(out_refs)
    act = activation(part_ref, recv_ref, hidden - split, scale_ref[:, 0:1])
    outs = [sum_ref[a] + dot(act, w_ref[a, split:]) for a in range(groups)]
    for d, out_ref in zip((0, *range(len(out_refs) - 1, 0, -1)), out_refs):
        rows = [out[d * capacity : (d + 1) * capacity] for out in outs]
        out_ref[...] = jnp.concatenate(rows, 0).astype(BF)


def down(split, part, recv, weights, sums, scale, count):
    groups, _, piece = weights.shape
    rows = part.shape[0] // count * groups
    return pl.pallas_call(
        functools.partial(down_kernel, split),
        in_specs=whole_vmem(5),
        out_specs=whole_vmem(count),
        out_shape=[in_vmem((rows, piece), BF)] * count,
        compiler_params=params(),
        name="down",
    )(part, recv, weights, sums, scale)


def combine_kernel(count, high_ref, low_ref, after_ref, *refs):
    del after_ref
    y_refs, out_refs, total = refs[:count], refs[count:-1], refs[-1]
    me = lax.axis_index("heads")
    groups = total.shape[0]
    capacity = y_refs[0].shape[0] // groups
    ys = [y_ref[...].astype(F32) for y_ref in (y_refs[0], *y_refs[:0:-1])]
    for a in range(groups):
        y = jnp.concatenate([y[a * capacity : (a + 1) * capacity] for y in ys], 0).astype(BF)
        total[a] = dot(high_ref[...], y) + dot(low_ref[...], y)
    for k, out_ref in zip((0, *range(groups - 1, 0, -1)), out_refs):
        out_ref[...] = total[me ^ k].astype(out_ref.dtype)


def combine(high, low, after, ys, groups):
    rows, piece = high.shape[0], ys[0].shape[1]
    return pl.pallas_call(
        functools.partial(combine_kernel, len(ys)),
        in_specs=whole_vmem(2) + [pl.BlockSpec(memory_space=pl.ANY)] + whole_vmem(len(ys)),
        out_specs=whole_vmem(groups),
        out_shape=[struct((rows, piece), F32)] + [struct((rows, piece), BF)] * (groups - 1),
        scratch_shapes=[pltpu.VMEM((groups, rows, piece), F32)],
        compiler_params=params(),
        name="combine",
    )(high, low, after, *ys)


def finish_kernel(own_ref, *refs):
    recv_refs, out_ref = refs[:-1], refs[-1]
    total = own_ref[...]
    for recv_ref in recv_refs:
        total = total + recv_ref[...].astype(F32)
    out_ref[...] = total.astype(BF).reshape(out_ref.shape)


def finish(own, recvs, shape):
    return pl.pallas_call(
        finish_kernel,
        in_specs=whole_vmem(1 + len(recvs)),
        out_specs=pl.BlockSpec(memory_space=pltpu.VMEM),
        out_shape=struct(shape, BF),
        compiler_params=params(),
        name="finish",
    )(own, *recvs)


def swap(x, axis, k):
    size = lax.axis_size(axis)
    return lax.ppermute(x, axis, [(i, i ^ k) for i in range(size)])


def swaps(sends, axis):
    return [swap(x, axis, k) for k, x in zip(range(len(sends), 0, -1), sends)]


def cross_swaps(sends):
    size = lax.axis_size("heads")
    return [
        lax.ppermute(
            x, ("heads", "side"), [(2 * i + s, 2 * (i ^ k) + 1 - s) for i in range(size) for s in (0, 1)]
        )
        for k, x in zip(range(len(sends), 0, -1), sends)
    ]


def local(
    queries, new_keys, new_values, head_states, slopes, head_gain, out_weight, residual,
    norm_gain, expert_ids, expert_gates, w_gate, w_up, w_down,
):
    groups, count = lax.axis_size("heads"), lax.axis_size("dp")
    width = norm_gain.shape[0]
    other, normed, states, weight = attention(
        slopes, queries, new_keys, new_values, head_states,
        head_gain.reshape(1, -1), out_weight, groups,
    )
    mine = project(out_weight, normed, weight, other.shape)
    own, *sends = split(mine, swap(other, "side", 1))
    weights = regroup(w_down, own)
    flat, *sends = add_residual(residual, weights, own, cross_swaps(sends))
    resid_out = by_request(flat, residual.shape)
    capacity = max(2, 3 * expert_ids.shape[2] * flat.shape[0] // (2 * count))
    pick, high, low = route(
        jnp.transpose(expert_ids, (1, 2, 0)), jnp.transpose(expert_gates, (1, 2, 0)), flat,
        capacity, count,
    )
    gathered = [flat] + swaps(sends, "heads")
    own, *sends = dispatch(pick, gathered, count)
    xs = [own] + swaps(sends, "dp")
    hidden = w_gate.shape[3]
    split_at = (hidden + 128) // 256 * 128
    part, lhs = first_units(split_at, norm_gain.reshape(1, -1), w_gate, w_up, xs)
    other_part = other_units(split_at, lhs, w_gate, w_up)
    sums, scale = down_first(width, split_at, part, swap(part, "side", 1), weights)
    own, *sends = down(
        split_at, other_part, swap(other_part, "side", 1), weights, sums, scale, count
    )
    state_out, done = new_state(slopes, new_keys, new_values, states, own)
    ys = [own] + swaps(sends, "dp")
    own, *sends = combine(high, low, done, ys, groups)
    return state_out, resid_out, finish(own, swaps(sends, "heads"), residual.shape)


def solution(mesh):
    return jax.shard_map(
        local,
        mesh=mesh,
        in_specs=(
            P("dp", None, ("heads", "side")),
            P("dp", None, ("heads", "side")),
            P("dp", None, ("heads", "side")),
            P("dp", ("heads", "side"), None, None),
            P(("heads", "side")),
            P(("heads", "side")),
            P(("heads", "side"), None),
            P("dp", None, ("heads", "side")),
            P(),
            P("dp", None, None),
            P("dp", None, None),
            P("dp", None, "side", "heads"),
            P("dp", None, "side", "heads"),
            P("dp", "heads", None, "side"),
        ),
        out_specs=(
            P("dp", ("heads", "side"), None, None),
            P("dp", None, ("heads", "side")),
            P("dp", None, ("heads", "side")),
        ),
        check_vma=False,
    )
```
